128 devices in a mesh: ep: 32 (over x, y, core), tp: 4 (over z).
Axes of the slice: x: 4, y: 4, z: 4, core: 2. Of those that a mesh axis runs over, the one named last changes fastest.
Arguments:
- tokens: bfloat16 [4096, 2560], P('ep'), may hold values from -6 to 6
- segments: int32 [4096], P('ep'), may hold values from 0 to 3, as said below
- routes: int32 [4096, 6], P('ep'), may hold values from 0 to 31, all different within a row; in each aligned block of 128 rows (0 to 127, 128 to 255, ...) at most 40 rows name the same one
- cotangent: bfloat16 [4096, 2560], P('ep'), may hold values from -6 to 6
- attn_gain: float32 [2560], replicated, may hold values from 0.5 to 1.5
- w_query: bfloat16 [2560, 2560], P(None, 'tp'), may hold values from -0.125 to 0.125
- key_weight: bfloat16 [2560, 512], P(None, 'tp'), may hold values from -0.125 to 0.125
- value_weight: bfloat16 [2560, 512], P(None, 'tp'), may hold values from -0.125 to 0.125
- w_out: bfloat16 [2560, 2560], P('tp'), may hold values from -1 to 1
- ffn_gain: float32 [2560], replicated, may hold values from 0.5 to 1.5
- w_router: bfloat16 [2560, 32], replicated, may hold values from -0.0625 to 0.0625
- shared_gate: bfloat16 [2560, 3072], P(None, 'tp'), may hold values from -0.125 to 0.125
- shared_up: bfloat16 [2560, 3072], P(None, 'tp'), may hold values from -0.125 to 0.125
- shared_down: bfloat16 [3072, 2560], P('tp'), may hold values from -0.15625 to 0.15625
- expert_gate: bfloat16 [32, 2560, 1536], P('ep', None, 'tp'), may hold values from -0.125 to 0.125
- expert_up: bfloat16 [32, 2560, 1536], P('ep', None, 'tp'), may hold values from -0.125 to 0.125
- expert_down: bfloat16 [32, 1536, 2560], P('ep', 'tp'), may hold values from -0.625 to 0.625
Outputs:
- output: bfloat16 [4096, 2560], P('ep')
- input_grad: float32 [4096, 2560], P('ep')
- attn_gain_grad: float32 [2560], P('ep')
- query_grad: float32 [2560, 2560], P('ep', 'tp')
- key_grad: float32 [2560, 512], P('ep', 'tp')
- value_grad: float32 [2560, 512], P('ep', 'tp')
- out_grad: float32 [2560, 2560], P('tp', 'ep')
- ffn_gain_grad: float32 [2560], P('ep')
- router_grad: float32 [2560, 32], P('ep')
- shared_gate_grad: float32 [2560, 3072], P('ep', 'tp')
- shared_up_grad: float32 [2560, 3072], P('ep', 'tp')
- shared_down_grad: float32 [3072, 2560], P('tp', 'ep')
- expert_gate_grad: float32 [32, 2560, 1536], P('ep', None, 'tp')
- expert_up_grad: float32 [32, 2560, 1536], P('ep', None, 'tp')
- expert_down_grad: float32 [32, 1536, 2560], P('ep', 'tp')
The draws below stay inside these ranges and needn't reach their ends.
Inputs may be any that keep to these rules, and one draw needn't show every extreme that they name: `segments`: the sequence holds 4 documents whose numbers never fall; each document's length is a multiple of 32 tokens. Document 0 ends within the first 128 tokens and documents 2 and 3 lie within the last 128 tokens, so document 1 runs from the first index of ep to the last. `routes`: each token names 6 different experts; among the 128 rows of one index of ep no expert is named more than 40 times.
All inputs are finite; a program needn't handle non-finite values.
Results may differ from the reference program's by a relative error of at most 0.025.
Values may be sent and summed in bfloat16 or wider, within the bound.
No kernel may reach another device: no remote copies, remote signals or barrier semaphores. Data moves between devices by JAX's collectives and lax.ppermute only.
A program may use at most 256 MiB of HBM per device.

```python
import math
import jax
import jax.numpy as jnp
import numpy as np
from jax import lax

MODEL_DIM = 2560
QUERY_HEADS = 20
KEY_VALUE_HEADS = 4
HEAD_DIM = 128
FF = 1536
TOPK = 6
TOK_DEV = 128
SFF = 3072
EXPERTS = 32
SEQUENCE_TOKENS = 4096
TOKENS = 4096
CAP = 40
N_EP = 32


def draw_segments(key, part):
    key = jax.random.fold_in(key, 7)
    key_first, key_second, key_third = jax.random.split(key, 3)
    unit_rows = TOK_DEV // 4
    first_units = jax.random.randint(key_first, (), 1, 4)
    second_units = jax.random.randint(key_second, (), 1, 3)
    third_units = jax.random.randint(key_third, (), 1, 4 - second_units)
    first_cut = first_units * unit_rows
    second_cut = SEQUENCE_TOKENS - (second_units + third_units) * unit_rows
    third_cut = SEQUENCE_TOKENS - third_units * unit_rows
    doc_cuts = jnp.stack([first_cut, second_cut, third_cut]).astype(jnp.int32)
    places = jnp.arange(SEQUENCE_TOKENS, dtype=jnp.int32)
    return jnp.sum((places[:, None] >= doc_cuts[None, :]).astype(jnp.int32), axis=-1).astype(jnp.int32)


def spiked(drawn, key, source, target, shards_of, factor):
    owner, partner = [(jnp.arange(drawn.shape[axis_at]) // (drawn.shape[axis_at] // shards_of)).reshape([-1 if axis == axis_at else 1 for axis in range(drawn.ndim)]) for axis_at in (source, target)]
    chosen = jax.random.permutation(key, shards_of)[partner]
    strong = (owner == chosen) | (owner == (partner + shards_of // 2) % shards_of)
    return jnp.where(strong, factor * drawn, drawn)


def block_levels(stream_key, shape, cuts, low, high):
    def one(position, shards_of):
        heights = jax.random.uniform(jax.random.fold_in(jax.random.fold_in(stream_key, 6), position), (shards_of,), jnp.float32, low / len(cuts), high / len(cuts))
        return jnp.repeat(jnp.exp(heights), shape[position] // shards_of).reshape((-1,) + (1,) * (len(shape) - position - 1))

    level = one(*cuts[0])
    for cut in cuts[1:]:
        level = level * one(*cut)
    return level


def routed_block(key, own, number, rows, number_of, top, reach, lean):
    ranking = jax.random.permutation(key, number_of)
    crowded, usual = shares(number_of, rows * top, reach, lean, True), shares(number_of, rows * top, reach, lean, False)
    places = jnp.arange(number_of)

    def named(lengths, rotation):
        used = int((lengths > 0).sum())
        fixed = max(1, used // 4)
        moved = fixed + (places - fixed + rotation * (used - fixed)) % max(1, number_of - fixed)
        return jnp.zeros((number_of,), jnp.int32).at[ranking[jnp.where(places < fixed, places, moved)]].set(jnp.asarray(lengths, jnp.int32))

    lengths = jnp.where(number % 4 == 0, named(crowded, number // 4), named(usual, number - number // 4 - 1))
    mixed = jax.random.permutation(jax.random.fold_in(own, 3), number_of)
    giver, sink = mixed[0:number_of // 2 * 2:2], mixed[1:number_of // 2 * 2:2]
    slack = jnp.minimum(lengths[giver] - 1, reach - lengths[sink]) // 2
    slack = jnp.where((giver == ranking[0]) | (sink == ranking[0]) | (lengths[sink] == 0), 0, jnp.maximum(slack, 0))
    moved = jax.random.randint(jax.random.fold_in(own, 4), (number_of // 2,), 0, 1 << 20) % (slack + 1)
    lengths = lengths.at[giver].add(-moved).at[sink].add(moved)
    members = jnp.searchsorted(jnp.cumsum(lengths), jnp.arange(rows * top), side="right").astype(jnp.int32)
    grid = members.reshape(top, rows).T
    grid = grid[jax.random.permutation(jax.random.fold_in(own, 1), rows)]
    rotation = jax.random.randint(jax.random.fold_in(own, 2), (rows, 1), 0, top)
    return jnp.take_along_axis(grid, (jnp.arange(top)[None, :] + rotation) % top, axis=1)


def shares(count, total, bound, skew, full):
    weights = [(1 << 20) // math.isqrt(rank ** skew) + 1 for rank in range(1, count + 1)]
    largest = bound if full else min(bound, max(-(-total // count), total * weights[0] // sum(weights)))
    least = 1 if total - largest >= count - 1 else 0
    holding, surplus = [largest] + [least] * (count - 1), total - largest - least * (count - 1)
    while surplus > 0:
        movable = [i for i in range(1, count) if holding[i] < largest] or [i for i in range(1, count) if holding[i] < bound]
        whole, remaining = sum([weights[i] for i in movable]), surplus
        for i in movable:
            addition = min(bound - holding[i], max(1, remaining * weights[i] // whole), surplus)
            holding[i] = holding[i] + addition
            surplus = surplus - addition
    return np.array(holding)


def scatter_about(own_key, shape, deviation, limit, pieces=(), kind=jnp.bfloat16):
    entries = jax.random.normal(own_key, shape, jnp.float32) * deviation
    if len(pieces) > 0:
        entries = block_levels(own_key, shape, pieces, -0.22, 0.18) * entries
    return jnp.clip(entries, min=-limit, max=limit).astype(kind)


def noise_with(key, dims, deviation, limit, cuts, heavy, held_as=jnp.bfloat16):
    result = deviation * jax.random.normal(key, dims, jnp.float32)
    if cuts:
        result = result * block_levels(key, dims, cuts, -0.22, 0.18)
    return jnp.clip(spiked(result, jax.random.fold_in(key, 3), *heavy), -limit, limit).astype(held_as)


def setup_inputs(seed: int = 0) -> dict:
    key_of = jax.random.split(jax.random.key(seed), 18)
    tokens = noise_with(key_of[0], (TOKENS, MODEL_DIM), 1.0, 6.0, ((0, 32),), (0, 1, 32, 2.75))
    segments = draw_segments(jax.random.fold_in(key_of[17], 71), 0)
    routes_keys = jax.random.split(jax.random.fold_in(key_of[2], 1), TOKENS // TOK_DEV)
    routes_turns = jax.random.permutation(jax.random.fold_in(key_of[2], 3), TOKENS // TOK_DEV)
    routes = jax.vmap(lambda own, number: routed_block(jax.random.fold_in(key_of[2], 2), own, number, TOK_DEV, EXPERTS, TOPK, CAP, 1))(routes_keys, routes_turns).reshape((TOKENS, TOPK))
    cotangent = noise_with(key_of[3], (TOKENS, MODEL_DIM), 1.0, 6.0, ((0, 32),), (0, 1, 32, 2.75))
    attn_gain = jnp.clip(1.0 + 0.1 * jax.random.normal(key_of[4], (MODEL_DIM,), jnp.float32), 0.5, 1.5)
    w_query = scatter_about(key_of[5], (MODEL_DIM, QUERY_HEADS * HEAD_DIM), MODEL_DIM ** -0.5, 0.125, ((1, 4),))
    key_weight = scatter_about(key_of[6], (MODEL_DIM, KEY_VALUE_HEADS * HEAD_DIM), MODEL_DIM ** -0.5, 0.125, ((1, 4),))
    value_weight = scatter_about(key_of[7], (MODEL_DIM, KEY_VALUE_HEADS * HEAD_DIM), MODEL_DIM ** -0.5, 0.125, ((1, 4),))
    w_out = scatter_about(key_of[8], (QUERY_HEADS * HEAD_DIM, MODEL_DIM), (QUERY_HEADS * HEAD_DIM // 64) ** -0.5, 1.0, ((0, 4),))
    ffn_gain = jnp.clip(1.0 + 0.1 * jax.random.normal(key_of[9], (MODEL_DIM,), jnp.float32), 0.5, 1.5)
    w_router = scatter_about(key_of[10], (MODEL_DIM, EXPERTS), (4 * MODEL_DIM) ** -0.5, 0.0625)
    shared_gate = scatter_about(key_of[11], (MODEL_DIM, SFF), MODEL_DIM ** -0.5, 0.125, ((1, 4),))
    shared_up = scatter_about(key_of[12], (MODEL_DIM, SFF), MODEL_DIM ** -0.5, 0.125, ((1, 4),))
    shared_down = scatter_about(key_of[13], (SFF, MODEL_DIM), (SFF // 2) ** -0.5, 0.15625, ((0, 4),))
    expert_gate = scatter_about(key_of[14], (EXPERTS, MODEL_DIM, FF), MODEL_DIM ** -0.5, 0.125, ((0, 32), (2, 4)))
    expert_up = scatter_about(key_of[15], (EXPERTS, MODEL_DIM, FF), MODEL_DIM ** -0.5, 0.125, ((0, 32), (2, 4)))
    expert_down = scatter_about(key_of[16], (EXPERTS, FF, MODEL_DIM), (FF // 16) ** -0.5, 0.625, ((0, 32), (1, 4)))
    return dict(tokens=tokens, segments=segments, routes=routes, cotangent=cotangent, attn_gain=attn_gain, w_query=w_query, key_weight=key_weight, value_weight=value_weight, w_out=w_out, ffn_gain=ffn_gain, w_router=w_router, shared_gate=shared_gate, shared_up=shared_up, shared_down=shared_down, expert_gate=expert_gate, expert_up=expert_up, expert_down=expert_down)


@jax.custom_vjp
def reduced_precision(v):
    return lax.optimization_barrier(v.astype(jnp.bfloat16)).astype(jnp.float32)

@jax.custom_vjp
def reduced_backward(v):
    return v

def low_keep(v):
    return (reduced_precision(v), None)

def low_pass(kept, grad):
    return (grad,)

def back_keep(v):
    return (v, None)

def back_low(kept, grad):
    return (reduced_precision(grad),)
reduced_precision.defvjp(low_keep, low_pass)
reduced_backward.defvjp(back_keep, back_low)
eps_norm = 1e-05
rope_base = 500000.0
highest = lax.Precision.HIGHEST
masked_score = -1e+30

def matrix_product(left_side, right_side):
    return jnp.dot(left_side, right_side, precision=highest, preferred_element_type=jnp.float32)

def rms_norm(values, gain):
    return values * lax.rsqrt(lax.optimization_barrier(jnp.mean(values * values, axis=-1, keepdims=True)) + eps_norm) * gain

def rotary(positions, head_size):
    half_size = head_size // 2
    inverse = jnp.power(rope_base, -2.0 * jnp.arange(half_size, dtype=jnp.float32) / head_size)
    angle = positions.astype(jnp.float32)[:, None] * inverse[None, :]
    return (jnp.cos(angle), jnp.sin(angle))

def rotate_pairs(values, cosine, sine):
    half_size = values.shape[-1] // 2
    lower_half = values[..., :half_size]
    upper_half = values[..., half_size:]
    return jnp.concatenate([lower_half * cosine - upper_half * sine, upper_half * cosine + lower_half * sine], axis=-1)

def expert_block(operands):
    slot_rows, gate_matrix, up_matrix, down_matrix = operands
    gate_act = reduced_backward(matrix_product(slot_rows, gate_matrix))
    up_act = reduced_backward(matrix_product(slot_rows, up_matrix))
    hidden_act = reduced_precision(jax.nn.silu(gate_act) * up_act)
    return reduced_backward(reduced_precision(matrix_product(hidden_act, down_matrix)))

def block_forward(seq_input, params, seq_seg, seq_route):
    attn_gain, w_query, key_weight, value_weight, w_out, ffn_gain, w_router, shared_gate, shared_up, shared_down, expert_gate, expert_up, expert_down = params
    heads_per_group = QUERY_HEADS // KEY_VALUE_HEADS
    score_scale = HEAD_DIM ** (-0.5)
    places = jnp.arange(SEQUENCE_TOKENS, dtype=jnp.int32)
    cosine, sine = rotary(places, HEAD_DIM)
    cosine = cosine[:, None, :]
    sine = sine[:, None, :]
    first_hidden = reduced_precision(rms_norm(seq_input, attn_gain))
    query_raw = reduced_backward(matrix_product(first_hidden, w_query)).reshape(SEQUENCE_TOKENS, QUERY_HEADS, HEAD_DIM)
    unrotated_key = reduced_backward(matrix_product(first_hidden, key_weight)).reshape(SEQUENCE_TOKENS, KEY_VALUE_HEADS, HEAD_DIM)
    query_rotated = reduced_precision(rotate_pairs(query_raw, cosine, sine))
    key_rotated = reduced_precision(rotate_pairs(unrotated_key, cosine, sine))
    value_reduced = reduced_backward(reduced_precision(matrix_product(first_hidden, value_weight))).reshape(SEQUENCE_TOKENS, KEY_VALUE_HEADS, HEAD_DIM)
    allowed = (seq_seg[:, None] == seq_seg[None, :]) & (places[:, None] >= places[None, :])

    def group_attend(operands):
        query_group, key_group, value_group = operands
        raw_scores = reduced_backward(jnp.einsum('qgd,cd->gqc', query_group, key_group, precision=highest) * score_scale)
        raw_scores = jnp.where(allowed[None], raw_scores, masked_score)
        attn_prob = reduced_precision(jax.nn.softmax(raw_scores, axis=-1))
        return jnp.einsum('gqc,cd->qgd', attn_prob, value_group, precision=highest)
    grouped_heads = (query_rotated.reshape(SEQUENCE_TOKENS, KEY_VALUE_HEADS, heads_per_group, HEAD_DIM).transpose(1, 0, 2, 3), key_rotated.transpose(1, 0, 2), value_reduced.transpose(1, 0, 2))
    attended = lax.map(jax.checkpoint(group_attend), grouped_heads)
    heads_out = reduced_backward(reduced_precision(attended.transpose(1, 0, 2, 3).reshape(SEQUENCE_TOKENS, QUERY_HEADS * HEAD_DIM)))
    attn_out = reduced_backward(matrix_product(heads_out, w_out))
    mid_state = seq_input + attn_out
    hidden_two = reduced_precision(rms_norm(mid_state, ffn_gain))
    logits = matrix_product(hidden_two, w_router)
    gates = jax.nn.softmax(jnp.take_along_axis(logits, seq_route, axis=1), axis=-1)
    shared_g = reduced_backward(matrix_product(hidden_two, shared_gate))
    shared_u = reduced_backward(matrix_product(hidden_two, shared_up))
    shared_act = reduced_precision(jax.nn.silu(shared_g) * shared_u)
    shared_out = reduced_backward(matrix_product(shared_act, shared_down))
    seq_cap = N_EP * CAP
    route_mask = (seq_route[:, :, None] == jnp.arange(EXPERTS, dtype=jnp.int32)[None, None, :]).astype(jnp.int32)
    per_token = lax.optimization_barrier(jnp.sum(route_mask, axis=1))
    rank = jnp.cumsum(per_token, axis=0) - per_token
    slot_pos = lax.optimization_barrier(jnp.sum(route_mask * rank[:, None, :], axis=-1))
    slot_index = (seq_route * seq_cap + slot_pos).reshape(-1).astype(jnp.int32)
    copies = jnp.stack([reduced_backward(hidden_two) for copy_index in range(TOPK)], axis=1).reshape(SEQUENCE_TOKENS * TOPK, MODEL_DIM)
    buffer = jnp.zeros((EXPERTS * seq_cap, MODEL_DIM), jnp.float32).at[slot_index].set(copies).reshape(EXPERTS, seq_cap, MODEL_DIM)
    expert_out = lax.map(jax.checkpoint(expert_block), (buffer, expert_gate, expert_up, expert_down)).reshape(EXPERTS * seq_cap, MODEL_DIM)
    picked = expert_out[slot_index].reshape(SEQUENCE_TOKENS, TOPK, MODEL_DIM)
    routed = lax.optimization_barrier(jnp.sum(gates[:, :, None] * picked, axis=1))
    return mid_state + shared_out + routed

def reference(tokens, segments, routes, cotangent, attn_gain, w_query, key_weight, value_weight, w_out, ffn_gain, w_router, shared_gate, shared_up, shared_down, expert_gate, expert_up, expert_down):
    weight_list = tuple((weight_arg.astype(jnp.float32) for weight_arg in (attn_gain, w_query, key_weight, value_weight, w_out, ffn_gain, w_router, shared_gate, shared_up, shared_down, expert_gate, expert_up, expert_down)))
    seq_count = TOKENS // SEQUENCE_TOKENS
    seq_tokens = tokens.astype(jnp.float32).reshape(seq_count, SEQUENCE_TOKENS, MODEL_DIM)
    seq_cots = cotangent.astype(jnp.float32).reshape(seq_count, SEQUENCE_TOKENS, MODEL_DIM)
    seq_segs = segments.reshape(seq_count, SEQUENCE_TOKENS)
    seq_routes = routes.reshape(seq_count, SEQUENCE_TOKENS, TOPK)

    def seq_step(totals, seq_item):
        seq_input, seq_seg, seq_route, seq_cot = seq_item

        def forward(layer_input, *params):
            return block_forward(layer_input, params, seq_seg, seq_route)
        seq_out, pull_back = jax.vjp(forward, seq_input, *weight_list)
        grad_list = pull_back(seq_cot)
        new_totals = tuple((total_part + grad_part for total_part, grad_part in zip(totals, grad_list[1:])))
        return (new_totals, (seq_out.astype(jnp.bfloat16), grad_list[0]))
    start = tuple((jnp.zeros_like(weight_arg) for weight_arg in weight_list))
    totals, (outputs, input_grads) = lax.scan(seq_step, start, (seq_tokens, seq_segs, seq_routes, seq_cots))
    return (outputs.reshape(TOKENS, MODEL_DIM), input_grads.reshape(TOKENS, MODEL_DIM), totals[0], totals[1], totals[2], totals[3], totals[4], totals[5], totals[6], totals[7], totals[8], totals[9], totals[10], totals[11], totals[12])
```

```python
import math

import jax
import jax.numpy as jnp
from jax import lax
from jax.experimental import pallas as pl
from jax.experimental.pallas import tpu as pltpu
from jax.sharding import Mesh
from jax.sharding import PartitionSpec as P

HEAD_DIM = 128
EP = ("x", "y", "core")
TP = "tp"

eps_norm = 1e-05
rope_base = 500000.0
masked_score = -1e30

bf16 = jnp.bfloat16
f32 = jnp.float32


def dot_plain(left, right):
    return jnp.dot(left, right, preferred_element_type=f32)


def dot_last(left, right):
    dims = (((left.ndim - 1,), (right.ndim - 1,)), ((), ()))
    return lax.dot_general(left, right, dims, preferred_element_type=f32)


def dot_first(left, right):
    return lax.dot_general(left, right, (((0,), (0,)), ((), ())), preferred_element_type=f32)


def rotary(positions, head_size):
    half = head_size // 2
    inverse = jnp.power(rope_base, -2.0 * jnp.arange(half, dtype=f32) / head_size)
    angle = positions.astype(f32)[:, None] * inverse[None, :]
    return jnp.cos(angle), jnp.sin(angle)


def turn(values, cosine, sine, back=False):
    rows, width = values.shape
    per_head = values.reshape(rows, width // HEAD_DIM, 2, HEAD_DIM // 2)
    low, high = per_head[:, :, 0], per_head[:, :, 1]
    c, s = cosine[:, None, :], sine[:, None, :]
    if back:
        s = -s
    return jnp.stack([low * c - high * s, high * c + low * s], axis=2).reshape(rows, width)


def shift(values, axis, step):
    size = lax.axis_size(axis)
    return lax.ppermute(values, axis, [(i, (i + step) % size) for i in range(size)])


def exchange_ep(values):
    return lax.all_to_all(values, EP, 0, 0, tiled=True)


def tp_scatter_sum(part):
    count = lax.axis_size(TP)
    rows, width = part.shape
    pieces = part.astype(bf16).reshape(count, rows // count, width)
    got = lax.all_to_all(pieces, TP, 0, 0, tiled=True)
    return jnp.sum(got.astype(f32), axis=0)


def tp_gather(rows):
    return lax.all_gather(rows, TP, axis=0, tiled=True)


def tp_sum_small(value):
    total = value
    for step in range(1, lax.axis_size(TP)):
        total = total + shift(value, TP, step)
    return total


KV_ROWS = 144


def load_chunk(idx, kv_ref, chunk):
    x, y, core = idx[0], idx[1], idx[2]
    keys, values = [], []
    for yb in range(4):
        for cb in range(2):
            place = lax.bitwise_xor(core, cb) * 16 + ((y - yb) & 3) * 4 + ((x - chunk) & 3)
            keys.append(kv_ref[place, 0:128, 0:128])
            values.append(kv_ref[place, 0:128, 128:256])
    return jnp.concatenate(keys, axis=0), jnp.concatenate(values, axis=0)


def first_allowed(idx, kv_ref, start_ref):
    x, y, core = idx[0], idx[1], idx[2]
    place = core * 16 + (y & 3) * 4 + (x & 3)
    ahead = kv_ref[place, 128:144, 0:128][0:1].astype(f32).astype(jnp.int32)
    start = start_ref[0:1, :]
    return jnp.where(start < 0, ahead, start)


def chunk_mask(chunk, keys, start, query_ids):
    key_ids = chunk * keys + lax.broadcasted_iota(jnp.int32, (keys, 128), 0)
    return (key_ids >= start) & (key_ids <= query_ids)


def stack_heads(ref, heads):
    return jnp.concatenate([ref[:, h * 128 : (h + 1) * 128] for h in range(heads)], axis=0)


def attn_forward_kernel(heads, idx, q_ref, kv_ref, start_ref, o_ref, lse_ref):
    scale = HEAD_DIM ** (-0.5)
    wide = heads * 128
    ep = idx[3]
    queries = stack_heads(q_ref, heads)
    start = first_allowed(idx, kv_ref, start_ref)
    query_ids = ep * 128 + lax.broadcasted_iota(jnp.int32, (1, 128), 1)
    keys_per = 1024

    def step(chunk, carry):
        top, total, acc = carry
        keys, values = load_chunk(idx, kv_ref, chunk)
        scores = dot_last(keys, queries) * scale
        mask = chunk_mask(chunk, keys_per, start, query_ids)
        mask = jnp.concatenate([mask] * heads, axis=1)
        scores = jnp.where(mask, scores, masked_score)
        new_top = jnp.maximum(top, jnp.max(scores, axis=0, keepdims=True))
        prob = jnp.exp(scores - new_top)
        fade = jnp.exp(top - new_top)
        total = total * fade + jnp.sum(prob, axis=0, keepdims=True)
        acc = acc * fade + dot_first(values, prob.astype(bf16))
        return new_top, total, acc

    chunks = (ep * 128 + 127) // keys_per + 1
    top, total, acc = lax.fori_loop(
        0,
        chunks,
        step,
        (
            jnp.full((1, wide), masked_score, f32),
            jnp.zeros((1, wide), f32),
            jnp.zeros((HEAD_DIM, wide), f32),
        ),
    )
    out = acc / total
    for h in range(heads):
        o_ref[:, h * 128 : (h + 1) * 128] = out[:, h * 128 : (h + 1) * 128].T.astype(bf16)
    lse_ref[...] = jnp.broadcast_to(top + jnp.log(total), lse_ref.shape)


def attn_backward_kernel(
    heads, idx, q_ref, do_ref, o_ref, lse_ref, kv_ref, start_ref, dq_ref, dkv_ref
):
    scale = HEAD_DIM ** (-0.5)
    wide = heads * 128
    ep = idx[3]
    queries = stack_heads(q_ref, heads)
    douts = stack_heads(do_ref, heads)
    outs = stack_heads(o_ref, heads)
    lse = lse_ref[0:1, :]
    product = douts.astype(f32) * outs.astype(f32)
    high = product.astype(bf16)
    low = (product - high.astype(f32)).astype(bf16)
    ones = jnp.ones((16, HEAD_DIM), bf16)
    delta = (dot_last(ones, high) + dot_last(ones, low))[0:1, :]
    start = first_allowed(idx, kv_ref, start_ref)
    query_ids = ep * 128 + lax.broadcasted_iota(jnp.int32, (1, 128), 1)
    keys_per = 1024
    dkv_ref[...] = jnp.zeros_like(dkv_ref)

    def step(chunk, dq):
        keys, values = load_chunk(idx, kv_ref, chunk)
        scores = dot_last(keys, queries) * scale
        mask = chunk_mask(chunk, keys_per, start, query_ids)
        mask = jnp.concatenate([mask] * heads, axis=1)
        prob = jnp.where(mask, jnp.exp(scores - lse), 0.0)
        dprob = dot_last(values, douts)
        dscore = (prob * (dprob - delta) * scale).astype(bf16)
        place = pl.ds(pl.multiple_of(chunk * keys_per, keys_per), keys_per)
        dkv_ref[place, 0:128] = dot_plain(dscore, queries).astype(bf16)
        dkv_ref[place, 128:256] = dot_plain(prob.astype(bf16), douts).astype(bf16)
        return dq + dot_first(keys, dscore)

    chunks = (ep * 128 + 127) // keys_per + 1
    dq = lax.fori_loop(0, chunks, step, jnp.zeros((HEAD_DIM, wide), f32))
    for h in range(heads):
        dq_ref[:, h * 128 : (h + 1) * 128] = dq[:, h * 128 : (h + 1) * 128].T


VMEM = pl.BlockSpec(memory_space=pltpu.VMEM)
SMEM = pl.BlockSpec(memory_space=pltpu.SMEM)
MIB = 1024 * 1024


def attn_forward(idx, q, kv, start):
    heads = q.shape[1] // HEAD_DIM
    return pl.pallas_call(
        lambda *refs: attn_forward_kernel(heads, *refs),
        out_shape=(
            jax.ShapeDtypeStruct(q.shape, bf16),
            jax.ShapeDtypeStruct((8, q.shape[1]), f32),
        ),
        in_specs=[SMEM, VMEM, VMEM, VMEM],
        out_specs=(VMEM, VMEM),
        compiler_params=pltpu.CompilerParams(vmem_limit_bytes=40 * MIB),
        cost_estimate=pl.CostEstimate(
            flops=4 * 2048 * 128 * q.shape[1], bytes_accessed=3 * MIB, transcendentals=2048 * 640
        ),
        name="attn_forward",
    )(idx, q, kv, start)


def attn_backward(idx, q, do, o, lse, kv, start, all_tokens):
    heads = q.shape[1] // HEAD_DIM
    return pl.pallas_call(
        lambda *refs: attn_backward_kernel(heads, *refs),
        out_shape=(
            jax.ShapeDtypeStruct(q.shape, f32),
            jax.ShapeDtypeStruct((all_tokens, 2 * HEAD_DIM), bf16),
        ),
        in_specs=[SMEM] + [VMEM] * 6,
        out_specs=(VMEM, VMEM),
        compiler_params=pltpu.CompilerParams(vmem_limit_bytes=40 * MIB),
        cost_estimate=pl.CostEstimate(
            flops=10 * 2048 * 128 * q.shape[1], bytes_accessed=5 * MIB, transcendentals=2048 * 640
        ),
        name="attn_backward",
    )(idx, q, do, o, lse, kv, start)


EXPERT_ROWS = 256
RIDER = 128


def expert_kernel(x_ref, u_ref, w_ref, ea_ref, dgu_ref, din_ref):
    ff = ea_ref.shape[1]
    width = x_ref.shape[1]
    both = dot_plain(x_ref[...], w_ref[...])
    gate, up = both[:, :ff], both[:, ff:]
    sig = 1.0 / (1.0 + jnp.exp(-gate))
    silu = gate * sig
    act = silu * up
    ea_ref[...] = act.astype(bf16)
    dact = u_ref[...]
    dup = dact * silu
    dgate = dact * up * (sig * (1.0 + gate * (1.0 - sig)))
    dboth = jnp.concatenate([dgate, dup], axis=1).astype(bf16)
    dgu_ref[...] = dboth
    din_ref[:, :width] = dot_last(dboth, w_ref[...]).astype(bf16)
    dgates = jnp.sum(dact * act, axis=1, keepdims=True)
    high = dgates.astype(bf16).astype(f32)
    lane = lax.broadcasted_iota(jnp.int32, (x_ref.shape[0], RIDER), 1)
    rider = jnp.where(lane == 0, high, jnp.where(lane == 1, dgates - high, 0.0))
    din_ref[:, width:] = rider.astype(bf16)


def expert_main(x, u, w_both):
    rows, width = x.shape
    ff = u.shape[1]
    steps = rows // EXPERT_ROWS
    return pl.pallas_call(
        expert_kernel,
        grid=(steps,),
        out_shape=(
            jax.ShapeDtypeStruct((rows, ff), bf16),
            jax.ShapeDtypeStruct((rows, 2 * ff), bf16),
            jax.ShapeDtypeStruct((rows, width + RIDER), bf16),
        ),
        in_specs=[
            pl.BlockSpec((EXPERT_ROWS, width), lambda i: (i, 0)),
            pl.BlockSpec((EXPERT_ROWS, ff), lambda i: (i, 0)),
            pl.BlockSpec((width, 2 * ff), lambda i: (0, 0)),
        ],
        out_specs=(
            pl.BlockSpec((EXPERT_ROWS, ff), lambda i: (i, 0)),
            pl.BlockSpec((EXPERT_ROWS, 2 * ff), lambda i: (i, 0)),
            pl.BlockSpec((EXPERT_ROWS, width + RIDER), lambda i: (i, 0)),
        ),
        compiler_params=pltpu.CompilerParams(vmem_limit_bytes=40 * MIB),
        cost_estimate=pl.CostEstimate(
            flops=8 * rows * width * ff, bytes_accessed=20 * MIB, transcendentals=rows * ff
        ),
        name="expert_main",
    )(x, u, w_both)


def body(
    tokens,
    segments,
    routes,
    cotangent,
    attn_gain,
    w_query,
    key_weight,
    value_weight,
    w_out,
    ffn_gain,
    w_router,
    shared_gate,
    shared_up,
    shared_down,
    expert_gate,
    expert_up,
    expert_down,
):
    rows, width = tokens.shape
    experts = w_router.shape[1]
    top = routes.shape[1]
    slots = min(rows, rows * top // experts * 5 // 3)
    tp_count = lax.axis_size(TP)
    tp = lax.axis_index(TP)
    ep_count = lax.axis_size(EP)
    ep = lax.axis_index(EP)
    own = rows // tp_count
    idx = jnp.stack(
        [lax.axis_index("x"), lax.axis_index("y"), lax.axis_index("core"), ep]
    ).astype(jnp.int32)

    def own_rows(array):
        return lax.dynamic_slice_in_dim(array, tp * own, own, axis=0)

    gate_mat, up_mat, down_mat = expert_gate[0], expert_up[0], expert_down[0]
    w_both = jnp.concatenate([gate_mat, up_mat], axis=1)

    cosine, sine = rotary(ep * rows + jnp.arange(rows, dtype=jnp.int32), HEAD_DIM)
    mask_et = jnp.sum(
        (routes.T[:, None, :] == jnp.arange(experts, dtype=jnp.int32)[None, :, None]).astype(f32),
        axis=0,
    )
    before = jnp.arange(rows)[:, None] < jnp.arange(rows)[None, :]
    rank_et = dot_plain(mask_et.astype(bf16), before.astype(bf16))
    place = (rank_et[:, None, :] == jnp.arange(slots, dtype=f32)[None, :, None]) & (
        mask_et[:, None, :] > 0.5
    )
    place_low = place.astype(bf16).reshape(experts * slots, rows)

    token_float = tokens.astype(f32)
    r1 = lax.rsqrt(jnp.mean(token_float * token_float, axis=-1, keepdims=True) + eps_norm)
    h1 = (token_float * r1 * attn_gain).astype(bf16)
    key = turn(dot_plain(h1, key_weight), cosine, sine).astype(bf16)
    value = dot_plain(h1, value_weight).astype(bf16)
    zeros_seen = jnp.sum((segments == 0).astype(f32))
    payload = jnp.concatenate(
        [
            jnp.concatenate([key, value], axis=1),
            jnp.broadcast_to(zeros_seen, (KV_ROWS - rows, 2 * HEAD_DIM)).astype(bf16),
        ],
        axis=0,
    )
    along_x = jnp.stack([payload] + [shift(payload, "x", k) for k in (1, 2, 3)])
    along_y = jnp.stack([along_x] + [shift(along_x, "y", k) for k in (1, 2, 3)])
    kv = jnp.stack([along_y, shift(along_y, "core", 1)]).reshape(ep_count, KV_ROWS, 2 * HEAD_DIM)
    query = turn(dot_plain(h1, w_query), cosine, sine).astype(bf16)
    below_two = jnp.sum((segments < 2).astype(jnp.int32))
    below_three = jnp.sum((segments < 3).astype(jnp.int32))
    start = jnp.where(
        segments == 0,
        0,
        jnp.where(
            segments == 1, -1, ep * rows + jnp.where(segments == 2, below_two, below_three)
        ),
    )
    start = jnp.broadcast_to(start.astype(jnp.int32)[None, :], (8, rows))

    g_out = dot_plain(place_low, cotangent).astype(bf16).reshape(experts, slots, width)
    g_in = exchange_ep(g_out).reshape(-1, width)
    u = dot_last(g_in, down_mat)

    heads_out, lse = attn_forward(idx, query, kv, start)
    x1 = own_rows(token_float) + tp_scatter_sum(dot_plain(heads_out, w_out))
    r2 = lax.rsqrt(jnp.mean(x1 * x1, axis=-1, keepdims=True) + eps_norm)
    h2 = tp_gather((x1 * r2 * ffn_gain).astype(bf16))

    h2_out = dot_plain(place_low, h2).astype(bf16).reshape(experts, slots, width)
    h2_in = exchange_ep(h2_out).reshape(-1, width)

    logits_et = lax.dot_general(
        w_router, h2, (((0,), (1,)), ((), ())), preferred_element_type=f32
    )
    masked = jnp.where(mask_et > 0.5, logits_et, masked_score)
    expo = jnp.where(
        mask_et > 0.5, jnp.exp(masked - jnp.max(masked, axis=0, keepdims=True)), 0.0
    )
    gate_et = expo / jnp.sum(expo, axis=0, keepdims=True)
    placed_gate = jnp.where(place, gate_et[:, None, :], 0.0)
    combine = placed_gate.astype(bf16).reshape(experts * slots, rows)
    gate_slots = jnp.sum(placed_gate, axis=2)
    gate_slots = jnp.pad(gate_slots, ((0, 0), (0, 128 - slots)))
    gate_sent = jnp.broadcast_to(gate_slots[:, None, :], (experts, 8, 128))
    gate_in = exchange_ep(gate_sent)[:, 0, :slots].reshape(-1, 1)

    shared_g = dot_plain(h2, shared_gate)
    shared_u = dot_plain(h2, shared_up)
    shared_sig = jax.nn.sigmoid(shared_g)
    shared_silu = shared_g * shared_sig
    shared_act = (shared_silu * shared_u).astype(bf16)
    shared_out = dot_plain(shared_act, shared_down)
    d_shared_act = dot_last(cotangent, shared_down)
    d_shared_g = (
        d_shared_act * shared_u * (shared_sig * (1.0 + shared_g * (1.0 - shared_sig)))
    ).astype(bf16)
    d_shared_u = (d_shared_act * shared_silu).astype(bf16)
    shared_grads = jnp.concatenate(
        [
            dot_first(h2, d_shared_g).astype(bf16),
            dot_first(h2, d_shared_u).astype(bf16),
            dot_first(cotangent, shared_act).astype(bf16),
        ],
        axis=1,
    )
    shared_sum = lax.psum_scatter(shared_grads, EP, scatter_dimension=0, tiled=True)
    d_two_shared = dot_last(d_shared_g, shared_gate) + dot_last(d_shared_u, shared_up)

    act, d_both, d_in = expert_main(h2_in, u, w_both)
    d_back = exchange_ep(d_in.reshape(ep_count, slots, width + RIDER))
    ff = act.shape[1]
    out_rows = dot_plain(act, down_mat).astype(bf16)
    out_back = exchange_ep(out_rows.reshape(ep_count, slots, width)).reshape(-1, width)
    expert_down_grad = dot_first((act.astype(f32) * gate_in).astype(bf16), g_in)[None]
    d_both_gated = (d_both.astype(f32) * gate_in).astype(bf16)
    expert_gate_grad = dot_first(h2_in, d_both_gated[:, :ff])[None]
    expert_up_grad = dot_first(h2_in, d_both_gated[:, ff:])[None]

    rider = d_back[:, :, width : width + 2].astype(f32)
    d_gate_slots = rider[:, :, 0] + rider[:, :, 1]
    d_gate_et = jnp.sum(jnp.where(place, d_gate_slots[:, :, None], 0.0), axis=1)
    d_logits_et = gate_et * (d_gate_et - jnp.sum(gate_et * d_gate_et, axis=0, keepdims=True))
    d_routed = dot_first(combine, d_back[:, :, :width].reshape(-1, width))
    d_router = lax.dot_general(
        d_logits_et.astype(bf16), w_router, (((0,), (1,)), ((), ())), preferred_element_type=f32
    )
    d_two = tp_scatter_sum(d_two_shared + d_routed + d_router)
    ffn_part = jnp.sum(d_two * x1 * r2, axis=0)
    scaled = ffn_gain * d_two
    d_x1 = (
        own_rows(cotangent).astype(f32)
        + r2 * scaled
        - x1 * (r2 * r2 * r2) * jnp.mean(scaled * x1, axis=-1, keepdims=True)
    )
    d_attn = tp_gather(d_x1.astype(bf16))

    d_heads = dot_last(d_attn, w_out).astype(bf16)
    d_query, d_kv = attn_backward(idx, query, d_heads, heads_out, lse, kv, start, ep_count * rows)
    d_kv = exchange_ep(d_kv.reshape(ep_count, rows, 2 * HEAD_DIM))
    d_kv = jnp.sum(d_kv.astype(f32), axis=0)
    d_key_raw = turn(d_kv[:, :HEAD_DIM], cosine, sine, back=True).astype(bf16)
    d_value = d_kv[:, HEAD_DIM:].astype(bf16)
    d_query_raw = turn(d_query, cosine, sine, back=True).astype(bf16)
    out_query_grads = jnp.concatenate(
        [
            dot_first(d_attn, heads_out).astype(bf16),
            dot_first(h1, d_query_raw).astype(bf16),
        ],
        axis=1,
    )
    out_query_sum = lax.psum_scatter(out_query_grads, EP, scatter_dimension=0, tiled=True)
    d_one = (
        dot_last(d_query_raw, w_query)
        + dot_last(d_key_raw, key_weight)
        + dot_last(d_value, value_weight)
    )
    d_one = tp_scatter_sum(d_one)
    own_tokens, own_r1 = own_rows(token_float), own_rows(r1)
    attn_part = jnp.sum(d_one * own_tokens * own_r1, axis=0)
    scaled_one = attn_gain * d_one
    input_rows = (
        d_x1
        + own_r1 * scaled_one
        - own_tokens
        * (own_r1 * own_r1 * own_r1)
        * jnp.mean(scaled_one * own_tokens, axis=-1, keepdims=True)
    )
    input_grad = tp_gather(input_rows.astype(bf16)).astype(f32)

    d_logits_all = tp_sum_small(d_logits_et).astype(bf16)
    router_part = lax.dot_general(
        h2, d_logits_all, (((0,), (1,)), ((), ())), preferred_element_type=f32
    )
    gains = tp_sum_small(jnp.stack([attn_part, ffn_part])).T
    gains_high = gains.astype(bf16).astype(f32)
    small = jnp.concatenate(
        [
            dot_first(h1, d_key_raw),
            dot_first(h1, d_value),
            router_part,
            gains_high,
            gains - gains_high,
            jnp.zeros((width, 128 - experts - 4), f32),
        ],
        axis=1,
    ).astype(bf16)
    small = exchange_ep(small.reshape(ep_count, width // ep_count, 3 * 128))
    small = jnp.sum(small.astype(f32), axis=0)
    gain_at = 2 * HEAD_DIM + experts

    routed = dot_first(combine, out_back)
    out_rows_own = x1 + tp_scatter_sum(shared_out + routed)
    output = tp_gather(out_rows_own.astype(bf16))

    sff = shared_g.shape[1]
    qw = query.shape[1]
    return (
        output,
        input_grad,
        small[:, gain_at] + small[:, gain_at + 2],
        out_query_sum[:, qw:].astype(f32),
        small[:, :HEAD_DIM],
        small[:, HEAD_DIM : 2 * HEAD_DIM],
        out_query_sum[:, :qw].astype(f32).T,
        small[:, gain_at + 1] + small[:, gain_at + 3],
        small[:, 2 * HEAD_DIM : gain_at],
        shared_sum[:, :sff].astype(f32),
        shared_sum[:, sff : 2 * sff].astype(f32),
        shared_sum[:, 2 * sff :].astype(f32).T,
        expert_gate_grad,
        expert_up_grad,
        expert_down_grad,
    )


def solution(mesh):
    ep_count, tp_count = mesh.shape["ep"], mesh.shape["tp"]
    side = math.isqrt(ep_count // 2)
    grid = Mesh(mesh.devices.reshape(side, side, 2, tp_count), EP + (TP,))
    return jax.shard_map(
        body,
        mesh=grid,
        in_specs=(
            P(EP, None),
            P(EP),
            P(EP, None),
            P(EP, None),
            P(),
            P(None, TP),
            P(None, TP),
            P(None, TP),
            P(TP, None),
            P(),
            P(),
            P(None, TP),
            P(None, TP),
            P(TP, None),
            P(EP, None, TP),
            P(EP, None, TP),
            P(EP, TP, None),
        ),
        out_specs=(
            P(EP, None),
            P(EP, None),
            P(EP),
            P(EP, TP),
            P(EP, TP),
            P(EP, TP),
            P(TP, EP),
            P(EP),
            P(EP, None),
            P(EP, TP),
            P(EP, TP),
            P(TP, EP),
            P(EP, None, TP),
            P(EP, None, TP),
            P(EP, TP, None),
        ),
        check_vma=False,
    )
```

```python
import math

import jax
import jax.numpy as jnp
from jax import lax
from jax.experimental import pallas as pl
from jax.experimental.pallas import tpu as pltpu
from jax.sharding import Mesh
from jax.sharding import PartitionSpec as P

HEAD_DIM = 128
EP = ("x", "y", "core")
TP = "tp"

eps_norm = 1e-05
rope_base = 500000.0
masked_score = -1e30

bf16 = jnp.bfloat16
f32 = jnp.float32

VMEM = pl.BlockSpec(memory_space=pltpu.VMEM)
SMEM = pl.BlockSpec(memory_space=pltpu.SMEM)
MIB = 1024 * 1024


def dot_plain(left, right):
    return jnp.dot(left, right, preferred_element_type=f32)


def dot_last(left, right):
    dims = (((left.ndim - 1,), (right.ndim - 1,)), ((), ()))
    return lax.dot_general(left, right, dims, preferred_element_type=f32)


def dot_first(left, right):
    return lax.dot_general(left, right, (((0,), (0,)), ((), ())), preferred_element_type=f32)


def struct(shape, dtype):
    return jax.ShapeDtypeStruct(shape, dtype)


def kernel_call(name, kernel, inputs, in_specs, out_shape, out_specs, flops=0, moved=0, **more):
    return pl.pallas_call(
        kernel,
        out_shape=out_shape,
        in_specs=in_specs,
        out_specs=out_specs,
        compiler_params=pltpu.CompilerParams(vmem_limit_bytes=40 * MIB),
        cost_estimate=pl.CostEstimate(flops=flops, bytes_accessed=moved, transcendentals=0),
        name=name,
        **more,
    )(*inputs)


def shift(values, axis, step):
    size = lax.axis_size(axis)
    return lax.ppermute(values, axis, [(i, (i + step) % size) for i in range(size)])


def exchange_ep(values):
    return lax.all_to_all(values, EP, 0, 0, tiled=True)


def tp_pieces(part, tp):
    count = lax.axis_size(TP)
    own = part.shape[0] // count
    got = []
    for step in range(1, count):
        piece = lax.dynamic_slice_in_dim(part, (tp + step) % count * own, own, axis=0)
        got.append(shift(piece, TP, step))
    return got


def tp_spread(rows):
    return [shift(rows, TP, step) for step in range(1, lax.axis_size(TP))]


def tp_sum_small(value):
    total = value
    for step in range(1, lax.axis_size(TP)):
        total = total + shift(value, TP, step)
    return total


def put_rows(target_ref, tp, pieces):
    own = pieces[0].shape[0]
    for step, piece in enumerate(pieces):
        at = ((tp - step) & 3) * own
        target_ref[pl.ds(pl.multiple_of(at, own), own), :] = piece[...].astype(target_ref.dtype)


def own_sum(tp, part_ref, got):
    own = got[0].shape[0]
    total = part_ref[pl.ds(pl.multiple_of(tp * own, own), own), :].astype(f32)
    for piece in got:
        total = total + piece[...].astype(f32)
    return total


KV_ROWS = 144


def rotated(values, cosine, sine):
    return values * cosine + pltpu.roll(values, HEAD_DIM // 2, 1) * sine


def norm_rows(values):
    return lax.rsqrt(jnp.mean(values * values, axis=-1, keepdims=True) + eps_norm)


def key_value_kernel(tok_ref, gain_ref, wk_ref, wv_ref, turn_ref, seg_ref, h1_ref, kv_ref):
    tok = tok_ref[...].astype(f32)
    h1 = (tok * norm_rows(tok) * gain_ref[...]).astype(bf16)
    h1_ref[...] = h1
    rows = tok.shape[0]
    key = rotated(dot_plain(h1, wk_ref[...]), turn_ref[0], turn_ref[1])
    kv_ref[0:rows, 0:HEAD_DIM] = key.astype(bf16)
    kv_ref[0:rows, HEAD_DIM:] = dot_plain(h1, wv_ref[...]).astype(bf16)
    zeros = jnp.sum((seg_ref[0:1, :] == 0).astype(f32), axis=1, keepdims=True)
    kv_ref[rows:, :] = jnp.broadcast_to(zeros, (KV_ROWS - rows, 2 * HEAD_DIM)).astype(bf16)


def query_kernel(h1_ref, wq_ref, turn_ref, q_ref):
    raw = dot_plain(h1_ref[...], wq_ref[...])
    for at in range(0, raw.shape[1], HEAD_DIM):
        head = raw[:, at : at + HEAD_DIM]
        q_ref[:, at : at + HEAD_DIM] = rotated(head, turn_ref[0], turn_ref[1]).astype(bf16)


CHUNK = 1024


def first_allowed(kv_ref, start_ref):
    start = start_ref[0:1, :]
    return jnp.where(start < 0, kv_ref[0:1, :].astype(jnp.int32), start)


def chunk_mask(chunk, start, query_ids, heads):
    key_ids = chunk * CHUNK + lax.broadcasted_iota(jnp.int32, (CHUNK, 128), 0)
    mask = (key_ids >= start) & (key_ids <= query_ids)
    return jnp.concatenate([mask] * heads, axis=1)


def stack_heads(values, heads):
    return jnp.concatenate([values[:, h * 128 : (h + 1) * 128] for h in range(heads)], axis=0)


def attn_forward_kernel(heads, idx, q_ref, start_ref, wo_ref, *refs):
    sources, (o_ref, lse_ref, kv_ref, ahead_ref, part_ref) = refs[:8], refs[8:]
    scale = HEAD_DIM ** (-0.5)
    wide = heads * 128
    x, y, core, ep = idx[0], idx[1], idx[2], idx[3]
    for near in range(2):
        for dy in range(4):
            source = sources[near * 4 + dy]
            for dx in range(4):
                block = ((x - dx) & 3) * 8 + ((y - dy) & 3) * 2 + (core ^ near)
                at = pl.ds(pl.multiple_of(block * 128, 128), 128)
                kv_ref[at, :] = source[dx * KV_ROWS : dx * KV_ROWS + 128, :]

                @pl.when(block == 0)
                def _():
                    row = source[dx * KV_ROWS + 128 : (dx + 1) * KV_ROWS, 0:128]
                    ahead_ref[...] = row[0:8].astype(f32)

    queries = stack_heads(q_ref[...], heads)
    start = first_allowed(ahead_ref, start_ref)
    query_ids = ep * 128 + lax.broadcasted_iota(jnp.int32, (1, 128), 1)

    def step(chunk, carry):
        top, total, acc = carry
        at = pl.ds(pl.multiple_of(chunk * CHUNK, CHUNK), CHUNK)
        keys, values = kv_ref[at, 0:128], kv_ref[at, 128:256]
        scores = dot_last(keys, queries) * scale
        scores = jnp.where(chunk_mask(chunk, start, query_ids, heads), scores, masked_score)
        new_top = jnp.maximum(top, jnp.max(scores, axis=0, keepdims=True))
        prob = jnp.exp(scores - new_top)
        fade = jnp.exp(top - new_top)
        total = total * fade + jnp.sum(prob, axis=0, keepdims=True)
        acc = acc * fade + dot_first(values, prob.astype(bf16))
        return new_top, total, acc

    chunks = (ep * 128 + 127) // CHUNK + 1
    top, total, acc = lax.fori_loop(
        0,
        chunks,
        step,
        (
            jnp.full((1, wide), masked_score, f32),
            jnp.zeros((1, wide), f32),
            jnp.zeros((HEAD_DIM, wide), f32),
        ),
    )
    out = acc / total
    out = jnp.concatenate(
        [out[:, h * 128 : (h + 1) * 128].T.astype(bf16) for h in range(heads)], axis=1
    )
    o_ref[...] = out
    lse_ref[...] = jnp.broadcast_to(top + jnp.log(total), lse_ref.shape)
    part_ref[...] = dot_plain(out, wo_ref[...]).astype(bf16)


def attn_backward_kernel(
    heads,
    idx,
    q_ref,
    o_ref,
    lse_ref,
    kv_ref,
    ahead_ref,
    start_ref,
    turn_ref,
    wo_ref,
    r0,
    r1,
    r2,
    r3,
    da_ref,
    dq_ref,
    dkv_ref,
):
    scale = HEAD_DIM ** (-0.5)
    wide = heads * 128
    ep, tp = idx[3], idx[4]
    put_rows(da_ref, tp, [r0, r1, r2, r3])
    d_heads = dot_last(da_ref[...], wo_ref[...]).astype(bf16)
    queries = stack_heads(q_ref[...], heads)
    douts = stack_heads(d_heads, heads)
    outs = stack_heads(o_ref[...], heads)
    lse = lse_ref[0:1, :]
    product = douts.astype(f32) * outs.astype(f32)
    high = product.astype(bf16)
    low = (product - high.astype(f32)).astype(bf16)
    ones = jnp.ones((16, HEAD_DIM), bf16)
    delta = (dot_last(ones, high) + dot_last(ones, low))[0:1, :]
    start = first_allowed(ahead_ref, start_ref)
    query_ids = ep * 128 + lax.broadcasted_iota(jnp.int32, (1, 128), 1)
    dkv_ref[...] = jnp.zeros_like(dkv_ref)

    def step(chunk, dq):
        at = pl.ds(pl.multiple_of(chunk * CHUNK, CHUNK), CHUNK)
        keys, values = kv_ref[at, 0:128], kv_ref[at, 128:256]
        scores = dot_last(keys, queries) * scale
        mask = chunk_mask(chunk, start, query_ids, heads)
        prob = jnp.where(mask, jnp.exp(scores - lse), 0.0)
        dprob = dot_last(values, douts)
        dscore = (prob * (dprob - delta) * scale).astype(bf16)
        dkv_ref[at, 0:128] = dot_plain(dscore, queries).astype(bf16)
        dkv_ref[at, 128:256] = dot_plain(prob.astype(bf16), douts).astype(bf16)
        return dq + dot_first(keys, dscore)

    chunks = (ep * 128 + 127) // CHUNK + 1
    dq = lax.fori_loop(0, chunks, step, jnp.zeros((HEAD_DIM, wide), f32))
    for h in range(heads):
        at = slice(h * 128, (h + 1) * 128)
        dq_ref[:, at] = rotated(dq[:, at].T, turn_ref[0], -turn_ref[1]).astype(bf16)


def mid_norm_kernel(idx, tok_ref, gain_ref, part_ref, g1, g2, g3, x1_ref, h2_ref):
    x1 = tok_ref[...].astype(f32) + own_sum(idx[4], part_ref, [g1, g2, g3])
    x1_ref[...] = x1
    h2_ref[...] = (x1 * norm_rows(x1) * gain_ref[...]).astype(bf16)


def place_kernel(idx, r0, r1, r2, r3, place_ref, h2_ref, slots_ref):
    @pl.when(pl.program_id(0) == 0)
    def _():
        put_rows(h2_ref, idx[4], [r0, r1, r2, r3])

    slots_ref[...] = dot_plain(place_ref[...], h2_ref[...]).astype(bf16)


EXPERT_ROWS = 256
RIDER = 128


def expert_kernel(x_ref, u_ref, w_ref, ea_ref, dgu_ref, din_ref):
    ff = ea_ref.shape[1]
    width = x_ref.shape[1]
    both = dot_plain(x_ref[...], w_ref[...])
    gate, up = both[:, :ff], both[:, ff:]
    sig = 1.0 / (1.0 + jnp.exp(-gate))
    silu = gate * sig
    act = silu * up
    ea_ref[...] = act.astype(bf16)
    dact = u_ref[...]
    dup = dact * silu
    dgate = dact * up * (sig * (1.0 + gate * (1.0 - sig)))
    dboth = jnp.concatenate([dgate, dup], axis=1).astype(bf16)
    dgu_ref[...] = dboth
    din_ref[:, :width] = dot_last(dboth, w_ref[...]).astype(bf16)
    dgates = jnp.sum(dact * act, axis=1, keepdims=True)
    high = dgates.astype(bf16).astype(f32)
    lane = lax.broadcasted_iota(jnp.int32, (x_ref.shape[0], RIDER), 1)
    rider = jnp.where(lane == 0, high, jnp.where(lane == 1, dgates - high, 0.0))
    din_ref[:, width:] = rider.astype(bf16)


def expert_main(x, u, w_both):
    rows, width = x.shape
    ff = u.shape[1]

    def rowed(columns):
        return pl.BlockSpec((EXPERT_ROWS, columns), lambda i: (i, 0))

    return kernel_call(
        "expert_main",
        expert_kernel,
        (x, u, w_both),
        [rowed(width), rowed(ff), pl.BlockSpec((width, 2 * ff), lambda i: (0, 0))],
        (
            struct((rows, ff), bf16),
            struct((rows, 2 * ff), bf16),
            struct((rows, width + RIDER), bf16),
        ),
        (rowed(ff), rowed(2 * ff), rowed(width + RIDER)),
        flops=8 * rows * width * ff,
        moved=20 * MIB,
        grid=(rows // EXPERT_ROWS,),
    )


COMBINE_COLUMNS = 512


def combine_kernel(
    combine_ref, place_ref, gate_ref, rider_ref, back_ref, shared_ref, router_ref, part_ref, dl_ref
):
    @pl.when(pl.program_id(0) == 0)
    def _():
        experts, rows = gate_ref.shape
        rider = rider_ref[...].astype(f32)
        value = rider[:, 0:1] + rider[:, 1:2]
        d_gate = place_ref[...].astype(f32) * value
        d_gate = jnp.sum(d_gate.reshape(experts, -1, rows), axis=1)
        gate = gate_ref[...]
        dl_ref[...] = gate * (d_gate - jnp.sum(gate * d_gate, axis=0, keepdims=True))

    total = dot_first(combine_ref[...], back_ref[...]) + shared_ref[...]
    total = total + dot_first(dl_ref[...].astype(bf16), router_ref[...])
    part_ref[...] = total.astype(bf16)


def combine_call(combine, place, gate, back, shared, router_t):
    slots, rows = combine.shape
    experts, width = router_t.shape
    cols = COMBINE_COLUMNS

    def whole(shape):
        return pl.BlockSpec(shape, lambda i: (0, 0))

    def tiled(height):
        return pl.BlockSpec((height, cols), lambda i: (0, i))

    return kernel_call(
        "combine_routes",
        combine_kernel,
        (combine, place, gate, back, back, shared, router_t),
        [
            whole((slots, rows)),
            whole((slots, rows)),
            whole((experts, rows)),
            pl.BlockSpec((slots, RIDER), lambda i: (0, width // RIDER)),
            tiled(slots),
            tiled(rows),
            tiled(experts),
        ],
        (struct((rows, width), bf16), struct((experts, rows), f32)),
        (tiled(rows), whole((experts, rows))),
        flops=2 * slots * rows * width,
        moved=8 * MIB,
        grid=(width // cols,),
    )


def mid_backward_kernel(
    idx, part_ref, g1, g2, g3, x1_ref, gain_ref, cot_ref, dx_ref, da_ref, gsum_ref
):
    d_two = own_sum(idx[4], part_ref, [g1, g2, g3])
    x1 = x1_ref[...]
    r2 = norm_rows(x1)
    gsum_ref[...] = jnp.broadcast_to(
        jnp.sum(d_two * x1 * r2, axis=0, keepdims=True), gsum_ref.shape
    )
    scaled = gain_ref[...] * d_two
    mean = jnp.mean(scaled * x1, axis=-1, keepdims=True)
    d_x1 = cot_ref[...].astype(f32) + r2 * scaled - x1 * (r2 * r2 * r2) * mean
    dx_ref[...] = d_x1
    da_ref[...] = d_x1.astype(bf16)


def first_backward_kernel(
    dkv_ref,
    turn_ref,
    wk_ref,
    wv_ref,
    dq_part_ref,
    tok_ref,
    dk_ref,
    dv_ref,
    part_ref,
    gsum_ref,
):
    total = jnp.sum(dkv_ref[...].astype(f32), axis=0)
    d_key = rotated(total[:, :HEAD_DIM], turn_ref[0], -turn_ref[1]).astype(bf16)
    d_value = total[:, HEAD_DIM:].astype(bf16)
    dk_ref[...] = d_key
    dv_ref[...] = d_value
    d_one = dq_part_ref[...] + dot_last(d_key, wk_ref[...]) + dot_last(d_value, wv_ref[...])
    part_ref[...] = d_one.astype(bf16)
    tok = tok_ref[...].astype(f32)
    gsum_ref[...] = jnp.broadcast_to(
        jnp.sum(d_one * tok * norm_rows(tok), axis=0, keepdims=True), gsum_ref.shape
    )


def input_rows_kernel(idx, part_ref, g1, g2, g3, tok_ref, gain_ref, dx_ref, out_ref):
    d_one = own_sum(idx[4], part_ref, [g1, g2, g3])
    tok = tok_ref[...].astype(f32)
    r1 = norm_rows(tok)
    scaled = gain_ref[...] * d_one
    mean = jnp.mean(scaled * tok, axis=-1, keepdims=True)
    out_ref[...] = (dx_ref[...] + r1 * scaled - tok * (r1 * r1 * r1) * mean).astype(bf16)


def output_rows_kernel(idx, part_ref, g1, g2, g3, x1_ref, out_ref):
    out_ref[...] = (x1_ref[...] + own_sum(idx[4], part_ref, [g1, g2, g3])).astype(bf16)


def assemble_kernel(idx, r0, r1, r2, r3, out_ref):
    put_rows(out_ref, idx[4], [r0, r1, r2, r3])


GRAD_ROWS = 256


def weight_grad_kernel(pairs, *refs):
    out_ref = refs[-1]
    at = 0
    cache = {}
    for left, rights in pairs:
        for right in rights:
            value = dot_first(refs[left][...], refs[right][...])
            columns = value.shape[1]
            key = (at, columns)
            cache[key] = value.astype(bf16)
            out_ref[:, at : at + columns] = cache[key]
            at += columns


def weight_grads(name, pairs):
    inputs, specs, plan, columns = [], [], [], 0
    width = pairs[0][0].shape[1]
    for left, rights in pairs:
        inputs.append(left)
        specs.append(pl.BlockSpec((left.shape[0], GRAD_ROWS), lambda i: (0, i)))
        left_at = len(inputs) - 1
        rights_at = []
        for right in rights:
            inputs.append(right)
            specs.append(pl.BlockSpec(right.shape, lambda i: (0, 0)))
            rights_at.append(len(inputs) - 1)
            columns += right.shape[1]
        plan.append((left_at, rights_at))
    return kernel_call(
        name,
        lambda *refs: weight_grad_kernel(plan, *refs),
        inputs,
        specs,
        struct((width, columns), bf16),
        pl.BlockSpec((GRAD_ROWS, columns), lambda i: (i, 0)),
        flops=2 * 128 * width * columns,
        moved=2 * width * columns,
        grid=(width // GRAD_ROWS,),
    )


def small_grad_kernel(h1_ref, dk_ref, dv_ref, h2_ref, dl_ref, gain_ref, pick_ref, out_ref):
    h1 = h1_ref[...]
    out_ref[:, 0:128] = dot_first(h1, dk_ref[...]).astype(bf16)
    out_ref[:, 128:256] = dot_first(h1, dv_ref[...]).astype(bf16)
    last = dot_first(h2_ref[...], dl_ref[...]) + dot_first(gain_ref[...], pick_ref[...])
    out_ref[:, 256:384] = last.astype(bf16)


def body(
    tokens,
    segments,
    routes,
    cotangent,
    attn_gain,
    w_query,
    key_weight,
    value_weight,
    w_out,
    ffn_gain,
    w_router,
    shared_gate,
    shared_up,
    shared_down,
    expert_gate,
    expert_up,
    expert_down,
):
    rows, width = tokens.shape
    experts = w_router.shape[1]
    top = routes.shape[1]
    slots = min(rows, rows * top // experts * 5 // 3)
    tp_count = lax.axis_size(TP)
    tp = lax.axis_index(TP)
    ep_count = lax.axis_size(EP)
    ep = lax.axis_index(EP)
    own = rows // tp_count
    quarter = width // tp_count
    qw = w_query.shape[1]
    heads = qw // HEAD_DIM
    all_tokens = ep_count * rows
    idx = jnp.stack(
        [lax.axis_index("x"), lax.axis_index("y"), lax.axis_index("core"), ep, tp]
    ).astype(jnp.int32)

    own_tokens = lax.dynamic_slice_in_dim(tokens, tp * own, own, axis=0)
    own_cot = lax.dynamic_slice_in_dim(cotangent, tp * own, own, axis=0)
    attn_row, ffn_row = attn_gain[None, :], ffn_gain[None, :]

    inverse = jnp.power(
        rope_base, -2.0 * jnp.arange(HEAD_DIM // 2, dtype=f32) / HEAD_DIM
    )
    angle = (ep * rows + jnp.arange(rows, dtype=jnp.int32)).astype(f32)[:, None] * inverse[None, :]
    cosine, sine = jnp.cos(angle), jnp.sin(angle)
    turn = jnp.stack(
        [jnp.concatenate([cosine, cosine], axis=1), jnp.concatenate([-sine, sine], axis=1)]
    )
    seg_rows = jnp.broadcast_to(segments[None, :], (8, rows))

    h1, payload = kernel_call(
        "key_value",
        key_value_kernel,
        (tokens, attn_row, key_weight, value_weight, turn, seg_rows),
        [VMEM] * 6,
        (struct((rows, width), bf16), struct((KV_ROWS, 2 * HEAD_DIM), bf16)),
        (VMEM, VMEM),
        flops=4 * rows * width * HEAD_DIM,
        moved=3 * MIB,
    )
    along_x = jnp.concatenate([payload] + [shift(payload, "x", k) for k in (1, 2, 3)], axis=0)
    along_y = [along_x] + [shift(along_x, "y", k) for k in (1, 2, 3)]
    across = [shift(block, "core", 1) for block in along_y]
    query = kernel_call(
        "query",
        query_kernel,
        (h1, w_query, turn),
        [VMEM] * 3,
        struct((rows, qw), bf16),
        VMEM,
        flops=2 * rows * width * qw,
        moved=5 * MIB,
    )
    below_two = jnp.sum((segments < 2).astype(jnp.int32))
    below_three = jnp.sum((segments < 3).astype(jnp.int32))
    start = jnp.where(
        segments == 0,
        0,
        jnp.where(
            segments == 1, -1, ep * rows + jnp.where(segments == 2, below_two, below_three)
        ),
    )
    start = jnp.broadcast_to(start.astype(jnp.int32)[None, :], (8, rows))

    mask_et = jnp.sum(
        (routes.T[:, None, :] == jnp.arange(experts, dtype=jnp.int32)[None, :, None]).astype(f32),
        axis=0,
    )
    before = jnp.arange(rows)[:, None] < jnp.arange(rows)[None, :]
    rank_et = dot_plain(mask_et.astype(bf16), before.astype(bf16))
    place = (rank_et[:, None, :] == jnp.arange(slots, dtype=f32)[None, :, None]) & (
        mask_et[:, None, :] > 0.5
    )
    place_low = place.astype(bf16).reshape(experts * slots, rows)
    own_columns = lax.dynamic_slice_in_dim(cotangent, tp * quarter, quarter, axis=1)
    g_out = dot_plain(place_low, own_columns).astype(bf16).reshape(experts, slots, quarter)

    heads_out, lse, kv, ahead, attn_part = kernel_call(
        "attn_forward",
        lambda *refs: attn_forward_kernel(heads, *refs),
        (idx, query, start, w_out, *along_y, *across),
        [SMEM] + [VMEM] * 11,
        (
            struct((rows, qw), bf16),
            struct((8, qw), f32),
            struct((all_tokens, 2 * HEAD_DIM), bf16),
            struct((8, 128), f32),
            struct((rows, width), bf16),
        ),
        (VMEM,) * 5,
        flops=4 * 2048 * 128 * qw,
        moved=12 * MIB,
    )
    g_out, attn_part = lax.optimization_barrier((g_out, attn_part))
    g_in = exchange_ep(g_out).reshape(-1, quarter)
    g_in = lax.all_gather(g_in, TP, axis=1, tiled=True)
    u = dot_last(g_in, expert_down[0])

    x1, h2_own = kernel_call(
        "mid_norm",
        mid_norm_kernel,
        (idx, own_tokens, ffn_row, attn_part, *tp_pieces(attn_part, tp)),
        [SMEM] + [VMEM] * 6,
        (struct((own, width), f32), struct((own, width), bf16)),
        (VMEM, VMEM),
        moved=2 * MIB,
    )

    def fixed(shape):
        return pl.BlockSpec(shape, lambda i: (0, 0))

    h2, h2_out = kernel_call(
        "place_rows",
        place_kernel,
        (idx, h2_own, *tp_spread(h2_own), place_low),
        [SMEM]
        + [fixed((own, width))] * 4
        + [pl.BlockSpec((EXPERT_ROWS, rows), lambda i: (i, 0))],
        (struct((rows, width), bf16), struct((experts * slots, width), bf16)),
        (fixed((rows, width)), pl.BlockSpec((EXPERT_ROWS, width), lambda i: (i, 0))),
        flops=2 * experts * slots * rows * width,
        moved=8 * MIB,
        grid=(experts * slots // EXPERT_ROWS,),
    )
    h2_in = exchange_ep(h2_out.reshape(experts, slots, width)).reshape(-1, width)

    logits_et = lax.dot_general(
        w_router, h2, (((0,), (1,)), ((), ())), preferred_element_type=f32
    )
    masked = jnp.where(mask_et > 0.5, logits_et, masked_score)
    expo = jnp.where(
        mask_et > 0.5, jnp.exp(masked - jnp.max(masked, axis=0, keepdims=True)), 0.0
    )
    gate_et = expo / jnp.sum(expo, axis=0, keepdims=True)
    placed_gate = jnp.where(place, gate_et[:, None, :], 0.0)
    combine = placed_gate.astype(bf16).reshape(experts * slots, rows)
    gate_slots = jnp.sum(placed_gate, axis=2)
    gate_slots = jnp.pad(gate_slots, ((0, 0), (0, 128 - slots)))
    gate_sent = jnp.broadcast_to(gate_slots[:, None, :], (experts, 8, 128))
    gate_in = exchange_ep(gate_sent)[:, 0, :slots].reshape(-1, 1)

    shared_g = dot_plain(h2, shared_gate)
    shared_u = dot_plain(h2, shared_up)
    shared_sig = jax.nn.sigmoid(shared_g)
    shared_silu = shared_g * shared_sig
    shared_act = (shared_silu * shared_u).astype(bf16)
    shared_out = dot_plain(shared_act, shared_down)
    d_shared_act = dot_last(cotangent, shared_down)
    d_shared_g = (
        d_shared_act * shared_u * (shared_sig * (1.0 + shared_g * (1.0 - shared_sig)))
    ).astype(bf16)
    d_shared_u = (d_shared_act * shared_silu).astype(bf16)
    shared_grads = weight_grads(
        "shared_grads", [(h2, [d_shared_g, d_shared_u]), (cotangent, [shared_act])]
    )
    shared_sum = lax.psum_scatter(shared_grads, EP, scatter_dimension=0, tiled=True)
    d_two_shared = dot_last(d_shared_g, shared_gate) + dot_last(d_shared_u, shared_up)
    w_both = jnp.concatenate([expert_gate[0], expert_up[0]], axis=1)
    h2_in, shared_grads, d_two_shared, w_both, u = lax.optimization_barrier(
        (h2_in, shared_grads, d_two_shared, w_both, u)
    )

    act, d_both, d_in = expert_main(h2_in, u, w_both)
    ff = act.shape[1]
    d_back = exchange_ep(d_in.reshape(ep_count, slots, width + RIDER))
    d_back = d_back.reshape(-1, width + RIDER)
    out_rows = dot_plain(act, expert_down[0]).astype(bf16)
    out_rows = lax.psum_scatter(out_rows, TP, scatter_dimension=1, tiled=True)
    expert_down_grad = dot_first((act.astype(f32) * gate_in).astype(bf16), g_in)[None]
    d_both_gated = (d_both.astype(f32) * gate_in).astype(bf16)
    expert_gate_grad = dot_first(h2_in, d_both_gated[:, :ff])[None]
    expert_up_grad = dot_first(h2_in, d_both_gated[:, ff:])[None]

    d_two_part, d_logits_et = combine_call(
        combine, place_low, gate_et, d_back, d_two_shared, w_router.T
    )
    d_x1, d_attn_own, ffn_part = kernel_call(
        "mid_backward",
        mid_backward_kernel,
        (idx, d_two_part, *tp_pieces(d_two_part, tp), x1, ffn_row, own_cot),
        [SMEM] + [VMEM] * 7,
        (struct((own, width), f32), struct((own, width), bf16), struct((8, width), f32)),
        (VMEM,) * 3,
        moved=2 * MIB,
    )

    d_attn, d_query_raw, d_kv = kernel_call(
        "attn_backward",
        lambda *refs: attn_backward_kernel(heads, *refs),
        (idx, query, heads_out, lse, kv, ahead, start, turn, w_out)
        + (d_attn_own, *tp_spread(d_attn_own)),
        [SMEM] + [VMEM] * 12,
        (
            struct((rows, width), bf16),
            struct((rows, qw), bf16),
            struct((all_tokens, 2 * HEAD_DIM), bf16),
        ),
        (VMEM,) * 3,
        flops=10 * 2048 * 128 * qw,
        moved=12 * MIB,
    )
    d_kv = exchange_ep(d_kv.reshape(ep_count, rows, 2 * HEAD_DIM))
    out_query_grads = weight_grads(
        "out_query_grads", [(d_attn, [heads_out]), (h1, [d_query_raw])]
    )
    out_query_sum = lax.psum_scatter(out_query_grads, EP, scatter_dimension=0, tiled=True)
    d_one_query = dot_last(d_query_raw, w_query)
    d_key_raw, d_value, d_one_part, attn_part_sum = kernel_call(
        "first_backward",
        first_backward_kernel,
        (d_kv, turn, key_weight, value_weight, d_one_query, tokens),
        [VMEM] * 6,
        (
            struct((rows, HEAD_DIM), bf16),
            struct((rows, HEAD_DIM), bf16),
            struct((rows, width), bf16),
            struct((8, width), f32),
        ),
        (VMEM,) * 4,
        flops=4 * rows * width * HEAD_DIM,
        moved=8 * MIB,
    )
    input_own = kernel_call(
        "input_rows",
        input_rows_kernel,
        (idx, d_one_part, *tp_pieces(d_one_part, tp), own_tokens, attn_row, d_x1),
        [SMEM] + [VMEM] * 7,
        struct((own, width), bf16),
        VMEM,
        moved=2 * MIB,
    )
    input_grad = kernel_call(
        "input_all",
        assemble_kernel,
        (idx, input_own, *tp_spread(input_own)),
        [SMEM] + [VMEM] * 4,
        struct((rows, width), f32),
        VMEM,
        moved=2 * MIB,
    )

    d_logits_all = tp_sum_small(d_logits_et).T.astype(bf16)
    d_logits_all = jnp.pad(d_logits_all, ((0, 0), (0, 128 - experts)))
    attn_total = tp_sum_small(attn_part_sum[0:1])
    ffn_total = tp_sum_small(ffn_part[0:1])
    attn_high, ffn_high = attn_total.astype(bf16), ffn_total.astype(bf16)
    gains = jnp.concatenate(
        [
            attn_high,
            ffn_high,
            (attn_total - attn_high.astype(f32)).astype(bf16),
            (ffn_total - ffn_high.astype(f32)).astype(bf16),
            jnp.zeros((12, width), bf16),
        ],
        axis=0,
    )
    pick = (
        jnp.arange(16, dtype=jnp.int32)[:, None] + experts
        == jnp.arange(128, dtype=jnp.int32)[None, :]
    ).astype(bf16)

    def strip(height):
        return pl.BlockSpec((height, GRAD_ROWS), lambda i: (0, i))

    small = kernel_call(
        "small_grads",
        small_grad_kernel,
        (h1, d_key_raw, d_value, h2, d_logits_all, gains, pick),
        [strip(rows), fixed((rows, 128)), fixed((rows, 128)), strip(rows), fixed((rows, 128))]
        + [strip(16), fixed((16, 128))],
        struct((width, 384), bf16),
        pl.BlockSpec((GRAD_ROWS, 384), lambda i: (i, 0)),
        flops=2 * rows * width * 384,
        moved=3 * MIB,
        grid=(width // GRAD_ROWS,),
    )
    small = exchange_ep(small.reshape(ep_count, width // ep_count, 384))
    small = jnp.sum(small.astype(f32), axis=0)
    gain_at = 2 * HEAD_DIM + experts

    out_back = exchange_ep(out_rows.reshape(ep_count, slots, quarter)).reshape(-1, quarter)
    routed = dot_first(combine, out_back)
    routed = lax.dynamic_update_slice_in_dim(
        jnp.zeros((rows, width), f32), routed, tp * quarter, axis=1
    )
    out_part = (shared_out + routed).astype(bf16)
    output_own = kernel_call(
        "output_rows",
        output_rows_kernel,
        (idx, out_part, *tp_pieces(out_part, tp), x1),
        [SMEM] + [VMEM] * 5,
        struct((own, width), bf16),
        VMEM,
        moved=2 * MIB,
    )
    output = kernel_call(
        "output_all",
        assemble_kernel,
        (idx, output_own, *tp_spread(output_own)),
        [SMEM] + [VMEM] * 4,
        struct((rows, width), bf16),
        VMEM,
        moved=2 * MIB,
    )

    sff = shared_g.shape[1]
    return (
        output,
        input_grad,
        small[:, gain_at] + small[:, gain_at + 2],
        out_query_sum[:, qw:].astype(f32),
        small[:, :HEAD_DIM],
        small[:, HEAD_DIM : 2 * HEAD_DIM],
        out_query_sum[:, :qw].astype(f32).T,
        small[:, gain_at + 1] + small[:, gain_at + 3],
        small[:, 2 * HEAD_DIM : gain_at],
        shared_sum[:, :sff].astype(f32),
        shared_sum[:, sff : 2 * sff].astype(f32),
        shared_sum[:, 2 * sff :].astype(f32).T,
        expert_gate_grad,
        expert_up_grad,
        expert_down_grad,
    )


def solution(mesh):
    ep_count, tp_count = mesh.shape["ep"], mesh.shape["tp"]
    side = math.isqrt(ep_count // 2)
    grid = Mesh(mesh.devices.reshape(side, side, 2, tp_count), EP + (TP,))
    return jax.shard_map(
        body,
        mesh=grid,
        in_specs=(
            P(EP, None),
            P(EP),
            P(EP, None),
            P(EP, None),
            P(),
            P(None, TP),
            P(None, TP),
            P(None, TP),
            P(TP, None),
            P(),
            P(),
            P(None, TP),
            P(None, TP),
            P(TP, None),
            P(EP, None, TP),
            P(EP, None, TP),
            P(EP, TP, None),
        ),
        out_specs=(
            P(EP, None),
            P(EP, None),
            P(EP),
            P(EP, TP),
            P(EP, TP),
            P(EP, TP),
            P(TP, EP),
            P(EP),
            P(EP, None),
            P(EP, TP),
            P(EP, TP),
            P(TP, EP),
            P(EP, None, TP),
            P(EP, None, TP),
            P(EP, TP, None),
        ),
        check_vma=False,
    )
```

```python
import math

import jax
import jax.numpy as jnp
from jax import lax
from jax.experimental import pallas as pl
from jax.experimental.pallas import tpu as pltpu
from jax.sharding import Mesh
from jax.sharding import PartitionSpec as P

HEAD_DIM = 128
EP = ("x", "y", "core")
CHIPS = ("x", "y")
TP = "tp"

eps_norm = 1e-05
rope_base = 500000.0
masked_score = -1e30

bf16 = jnp.bfloat16
f32 = jnp.float32

VMEM = pl.BlockSpec(memory_space=pltpu.VMEM)
SMEM = pl.BlockSpec(memory_space=pltpu.SMEM)
MIB = 1024 * 1024


def dot_plain(left, right):
    return jnp.dot(left, right, preferred_element_type=f32)


def dot_last(left, right):
    dims = (((left.ndim - 1,), (right.ndim - 1,)), ((), ()))
    return lax.dot_general(left, right, dims, preferred_element_type=f32)


def dot_first(left, right):
    return lax.dot_general(left, right, (((0,), (0,)), ((), ())), preferred_element_type=f32)


def struct(shape, dtype):
    return jax.ShapeDtypeStruct(shape, dtype)


def kernel_call(name, kernel, inputs, in_specs, out_shape, out_specs, flops=0, moved=0, **more):
    return pl.pallas_call(
        kernel,
        out_shape=out_shape,
        in_specs=in_specs,
        out_specs=out_specs,
        compiler_params=pltpu.CompilerParams(vmem_limit_bytes=48 * MIB),
        cost_estimate=pl.CostEstimate(flops=flops, bytes_accessed=moved, transcendentals=0),
        name=name,
        **more,
    )(*inputs)


def shift(values, axis, step):
    size = lax.axis_size(axis)
    return lax.ppermute(values, axis, [(i, (i + step) % size) for i in range(size)])


def exchange_ep(values):
    return lax.all_to_all(values, EP, 0, 0, tiled=True)


def tp_pieces(part, tp):
    count = lax.axis_size(TP)
    own = part.shape[0] // count
    got = []
    for step in range(1, count):
        piece = lax.dynamic_slice_in_dim(part, (tp + step) % count * own, own, axis=0)
        got.append(shift(piece, TP, step))
    return got


def tp_spread(rows):
    return [shift(rows, TP, step) for step in range(1, lax.axis_size(TP))]


def tp_sum_small(value):
    total = value
    for step in range(1, lax.axis_size(TP)):
        total = total + shift(value, TP, step)
    return total


def put_rows(target_ref, tp, pieces):
    own = pieces[0].shape[0]
    for step, piece in enumerate(pieces):
        at = ((tp - step) & 3) * own
        target_ref[pl.ds(pl.multiple_of(at, own), own), :] = piece[...].astype(target_ref.dtype)


def own_sum(tp, part_ref, got):
    own = got[0].shape[0]
    total = part_ref[pl.ds(pl.multiple_of(tp * own, own), own), :].astype(f32)
    for piece in got:
        total = total + piece[...].astype(f32)
    return total


KV_ROWS = 144


def rotated(values, cosine, sine):
    return values * cosine + pltpu.roll(values, HEAD_DIM // 2, 1) * sine


def norm_rows(values):
    return lax.rsqrt(jnp.mean(values * values, axis=-1, keepdims=True) + eps_norm)


def key_value_kernel(tok_ref, gain_ref, wk_ref, wv_ref, turn_ref, seg_ref, h1_ref, kv_ref):
    tok = tok_ref[...].astype(f32)
    h1 = (tok * norm_rows(tok) * gain_ref[...]).astype(bf16)
    h1_ref[...] = h1
    rows = tok.shape[0]
    key = rotated(dot_plain(h1, wk_ref[...]), turn_ref[0], turn_ref[1])
    kv_ref[0:rows, 0:HEAD_DIM] = key.astype(bf16)
    kv_ref[0:rows, HEAD_DIM:] = dot_plain(h1, wv_ref[...]).astype(bf16)
    zeros = jnp.sum((seg_ref[0:1, :] == 0).astype(f32), axis=1, keepdims=True)
    kv_ref[rows:, :] = jnp.broadcast_to(zeros, (KV_ROWS - rows, 2 * HEAD_DIM)).astype(bf16)


def query_kernel(h1_ref, wq_ref, turn_ref, q_ref):
    raw = dot_plain(h1_ref[...], wq_ref[...])
    for at in range(0, raw.shape[1], HEAD_DIM):
        head = raw[:, at : at + HEAD_DIM]
        q_ref[:, at : at + HEAD_DIM] = rotated(head, turn_ref[0], turn_ref[1]).astype(bf16)


CHUNK = 1024


def first_allowed(kv_ref, start_ref):
    start = start_ref[0:1, :]
    return jnp.where(start < 0, kv_ref[0:1, :].astype(jnp.int32), start)


def chunk_mask(chunk, start, query_ids, heads):
    key_ids = chunk * CHUNK + lax.broadcasted_iota(jnp.int32, (CHUNK, 128), 0)
    mask = (key_ids >= start) & (key_ids <= query_ids)
    return jnp.concatenate([mask] * heads, axis=1)


def stack_heads(values, heads):
    return jnp.concatenate([values[:, h * 128 : (h + 1) * 128] for h in range(heads)], axis=0)


def attn_forward_kernel(heads, idx, q_ref, start_ref, wo_ref, *refs):
    sources, (o_ref, lse_ref, kv_ref, ahead_ref, part_ref) = refs[:8], refs[8:]
    scale = HEAD_DIM ** (-0.5)
    wide = heads * 128
    x, y, core, ep = idx[0], idx[1], idx[2], idx[3]
    for near in range(2):
        for dy in range(4):
            source = sources[near * 4 + dy]
            for dx in range(4):
                block = ((x - dx) & 3) * 8 + ((y - dy) & 3) * 2 + (core ^ near)
                at = pl.ds(pl.multiple_of(block * 128, 128), 128)
                kv_ref[at, :] = source[dx * KV_ROWS : dx * KV_ROWS + 128, :]

                @pl.when(block == 0)
                def _():
                    row = source[dx * KV_ROWS + 128 : (dx + 1) * KV_ROWS, 0:128]
                    ahead_ref[...] = row[0:8].astype(f32)

    queries = stack_heads(q_ref[...], heads)
    start = first_allowed(ahead_ref, start_ref)
    query_ids = ep * 128 + lax.broadcasted_iota(jnp.int32, (1, 128), 1)

    def step(chunk, carry):
        top, total, acc = carry
        at = pl.ds(pl.multiple_of(chunk * CHUNK, CHUNK), CHUNK)
        keys, values = kv_ref[at, 0:128], kv_ref[at, 128:256]
        scores = dot_last(keys, queries) * scale
        scores = jnp.where(chunk_mask(chunk, start, query_ids, heads), scores, masked_score)
        new_top = jnp.maximum(top, jnp.max(scores, axis=0, keepdims=True))
        prob = jnp.exp(scores - new_top)
        fade = jnp.exp(top - new_top)
        total = total * fade + jnp.sum(prob, axis=0, keepdims=True)
        acc = acc * fade + dot_first(values, prob.astype(bf16))
        return new_top, total, acc

    chunks = (ep * 128 + 127) // CHUNK + 1
    top, total, acc = lax.fori_loop(
        0,
        chunks,
        step,
        (
            jnp.full((1, wide), masked_score, f32),
            jnp.zeros((1, wide), f32),
            jnp.zeros((HEAD_DIM, wide), f32),
        ),
    )
    out = acc / total
    out = jnp.concatenate(
        [out[:, h * 128 : (h + 1) * 128].T.astype(bf16) for h in range(heads)], axis=1
    )
    o_ref[...] = out
    lse_ref[...] = jnp.broadcast_to(top + jnp.log(total), lse_ref.shape)
    part_ref[...] = dot_plain(out, wo_ref[...]).astype(bf16)


def attn_backward_kernel(
    heads,
    idx,
    q_ref,
    o_ref,
    lse_ref,
    kv_ref,
    ahead_ref,
    start_ref,
    turn_ref,
    wo_ref,
    r0,
    r1,
    r2,
    r3,
    da_ref,
    dq_ref,
    dkv_ref,
):
    scale = HEAD_DIM ** (-0.5)
    wide = heads * 128
    ep, tp = idx[3], idx[4]
    put_rows(da_ref, tp, [r0, r1, r2, r3])
    d_heads = dot_last(da_ref[...], wo_ref[...]).astype(bf16)
    queries = stack_heads(q_ref[...], heads)
    douts = stack_heads(d_heads, heads)
    outs = stack_heads(o_ref[...], heads)
    lse = lse_ref[0:1, :]
    product = douts.astype(f32) * outs.astype(f32)
    high = product.astype(bf16)
    low = (product - high.astype(f32)).astype(bf16)
    ones = jnp.ones((16, HEAD_DIM), bf16)
    delta = (dot_last(ones, high) + dot_last(ones, low))[0:1, :]
    start = first_allowed(ahead_ref, start_ref)
    query_ids = ep * 128 + lax.broadcasted_iota(jnp.int32, (1, 128), 1)
    dkv_ref[...] = jnp.zeros_like(dkv_ref)

    def step(chunk, dq):
        at = pl.ds(pl.multiple_of(chunk * CHUNK, CHUNK), CHUNK)
        keys, values = kv_ref[at, 0:128], kv_ref[at, 128:256]
        scores = dot_last(keys, queries) * scale
        mask = chunk_mask(chunk, start, query_ids, heads)
        prob = jnp.where(mask, jnp.exp(scores - lse), 0.0)
        dprob = dot_last(values, douts)
        dscore = (prob * (dprob - delta) * scale).astype(bf16)
        dkv_ref[at, 0:128] = dot_plain(dscore, queries).astype(bf16)
        dkv_ref[at, 128:256] = dot_plain(prob.astype(bf16), douts).astype(bf16)
        return dq + dot_first(keys, dscore)

    chunks = (ep * 128 + 127) // CHUNK + 1
    dq = lax.fori_loop(0, chunks, step, jnp.zeros((HEAD_DIM, wide), f32))
    for h in range(heads):
        at = slice(h * 128, (h + 1) * 128)
        dq_ref[:, at] = rotated(dq[:, at].T, turn_ref[0], -turn_ref[1]).astype(bf16)


def mid_norm_kernel(idx, tok_ref, gain_ref, part_ref, g1, g2, g3, x1_ref, h2_ref):
    x1 = tok_ref[...].astype(f32) + own_sum(idx[4], part_ref, [g1, g2, g3])
    x1_ref[...] = x1
    h2_ref[...] = (x1 * norm_rows(x1) * gain_ref[...]).astype(bf16)


def place_kernel(idx, r0, r1, r2, r3, place_ref, h2_ref, slots_ref):
    @pl.when(pl.program_id(0) == 0)
    def _():
        put_rows(h2_ref, idx[4], [r0, r1, r2, r3])

    slots_ref[...] = dot_plain(place_ref[...], h2_ref[...]).astype(bf16)


EXPERT_ROWS = 640
EXPERT_PART = 320
PLACE_ROWS = 256
RIDER = 128


def expert_kernel(x_ref, u_ref, w_ref, ea_ref, dgu_ref, din_ref):
    ff = ea_ref.shape[1]
    width = x_ref.shape[1]
    for first in range(0, EXPERT_ROWS, EXPERT_PART):
        part = slice(first, first + EXPERT_PART)
        both = dot_plain(x_ref[part, :], w_ref[...])
        gate, up = both[:, :ff], both[:, ff:]
        sig = 1.0 / (1.0 + jnp.exp(-gate))
        silu = gate * sig
        act = silu * up
        ea_ref[part, :] = act.astype(bf16)
        dact = u_ref[part, :]
        dup = dact * silu
        dgate = dact * up * (sig * (1.0 + gate * (1.0 - sig)))
        dboth = jnp.concatenate([dgate, dup], axis=1).astype(bf16)
        dgu_ref[part, :] = dboth
        din_ref[part, :width] = dot_last(dboth, w_ref[...]).astype(bf16)
        dgates = jnp.sum(dact * act, axis=1, keepdims=True)
        high = dgates.astype(bf16).astype(f32)
        lane = lax.broadcasted_iota(jnp.int32, (EXPERT_PART, RIDER), 1)
        rider = jnp.where(lane == 0, high, jnp.where(lane == 1, dgates - high, 0.0))
        din_ref[part, width:] = rider.astype(bf16)


def cotangent_rows_kernel(idx, own_ref, before_ref, after_ref, top_ref, low_ref, down_ref, g_ref, u_ref):
    tp = idx[4]
    quarter = own_ref.shape[1]
    half = pl.num_programs(0) // 2

    def columns(owner):
        return pl.ds(pl.multiple_of((owner & 3) * quarter, 128), quarter)

    g_ref[:, columns(tp)] = own_ref[...]
    g_ref[:, columns(tp + 3)] = before_ref[...]
    g_ref[:, columns(tp + 1)] = after_ref[...]
    g_ref[:, columns(tp + 2)] = jnp.where(pl.program_id(0) < half, top_ref[...], low_ref[...])
    u_ref[...] = dot_last(g_ref[...], down_ref[...])


def cotangent_rows(idx, mine, down):
    slots, quarter = mine.shape
    ff, width = down.shape
    half = slots // 2
    before, after = shift(mine, TP, 1), shift(mine, TP, -1)
    top = shift(before[:half], TP, 1)
    low = shift(after[half:], TP, -1)
    step = 128
    steps = slots // step

    def rowed(columns):
        return pl.BlockSpec((step, columns), lambda i: (i, 0))

    return kernel_call(
        "cotangent_rows",
        cotangent_rows_kernel,
        (idx, mine, before, after, top, low, down),
        [
            SMEM,
            rowed(quarter),
            rowed(quarter),
            rowed(quarter),
            pl.BlockSpec((step, quarter), lambda i: (jnp.minimum(i, steps // 2 - 1), 0)),
            pl.BlockSpec((step, quarter), lambda i: (jnp.maximum(i - steps // 2, 0), 0)),
            pl.BlockSpec((ff, width), lambda i: (0, 0)),
        ],
        (struct((slots, width), bf16), struct((slots, ff), f32)),
        (rowed(width), rowed(ff)),
        flops=2 * slots * width * ff,
        moved=16 * MIB,
        grid=(steps,),
    )


def expert_out_kernel(idx, act_ref, down_ref, out_ref):
    out_ref[0] = dot_plain(act_ref[...], down_ref[...]).astype(bf16)


def expert_out(idx, act, down, pieces):
    slots, ff = act.shape
    quarter = down.shape[1] // pieces
    return pl.pallas_call(
        expert_out_kernel,
        out_shape=struct((pieces, slots, quarter), bf16),
        grid_spec=pltpu.PrefetchScalarGridSpec(
            num_scalar_prefetch=1,
            grid=(pieces, slots // EXPERT_ROWS),
            in_specs=[
                pl.BlockSpec((EXPERT_ROWS, ff), lambda k, i, idx: (i, 0)),
                pl.BlockSpec((ff, quarter), lambda k, i, idx: (0, (idx[4] + k) & 3)),
            ],
            out_specs=pl.BlockSpec((1, EXPERT_ROWS, quarter), lambda k, i, idx: (k, i, 0)),
        ),
        compiler_params=pltpu.CompilerParams(vmem_limit_bytes=32 * MIB),
        cost_estimate=pl.CostEstimate(
            flops=2 * slots * ff * quarter * pieces, bytes_accessed=9 * MIB, transcendentals=0
        ),
        name="expert_out",
    )(idx, act, down)


def expert_main(x, u, w_both):
    rows, width = x.shape
    ff = u.shape[1]

    def rowed(columns):
        return pl.BlockSpec((EXPERT_ROWS, columns), lambda i: (i, 0))

    return kernel_call(
        "expert_main",
        expert_kernel,
        (x, u, w_both),
        [rowed(width), rowed(ff), pl.BlockSpec((width, 2 * ff), lambda i: (0, 0))],
        (
            struct((rows, ff), bf16),
            struct((rows, 2 * ff), bf16),
            struct((rows, width + RIDER), bf16),
        ),
        (rowed(ff), rowed(2 * ff), rowed(width + RIDER)),
        flops=8 * rows * width * ff,
        moved=20 * MIB,
        grid=(rows // EXPERT_ROWS,),
    )


SHARED_COLUMNS = 256


def shared_kernel(
    h2_ref, cot_ref, gate_ref, up_ref, down_ref, act_ref, dg_ref, du_ref, out_ref, dh_ref
):
    gate = dot_plain(h2_ref[...], gate_ref[...])
    up = dot_plain(h2_ref[...], up_ref[...])
    dact = dot_last(cot_ref[...], down_ref[...])
    sig = 1.0 / (1.0 + jnp.exp(-gate))
    silu = gate * sig
    act = (silu * up).astype(bf16)
    dgate = (dact * up * (sig * (1.0 + gate * (1.0 - sig)))).astype(bf16)
    dup = (dact * silu).astype(bf16)
    act_ref[...] = act
    dg_ref[...] = dgate
    du_ref[...] = dup
    out = dot_plain(act, down_ref[...])
    dh = dot_last(dgate, gate_ref[...]) + dot_last(dup, up_ref[...])
    first = pl.program_id(0) == 0

    @pl.when(first)
    def _():
        out_ref[...] = out
        dh_ref[...] = dh

    @pl.when(jnp.logical_not(first))
    def _():
        out_ref[...] += out
        dh_ref[...] += dh


def shared_experts(h2, cotangent, gate, up, down):
    rows, width = h2.shape
    hidden = gate.shape[1]
    cols = SHARED_COLUMNS
    whole = pl.BlockSpec((rows, width), lambda i: (0, 0))
    column = pl.BlockSpec((width, cols), lambda i: (0, i))
    hid = pl.BlockSpec((rows, cols), lambda i: (0, i))
    return kernel_call(
        "shared_experts",
        shared_kernel,
        (h2, cotangent, gate, up, down),
        [whole, whole, column, column, pl.BlockSpec((cols, width), lambda i: (i, 0))],
        (struct((rows, hidden), bf16),) * 3 + (struct((rows, width), f32),) * 2,
        (hid, hid, hid, whole, whole),
        flops=14 * rows * width * hidden,
        moved=16 * MIB,
        grid=(hidden // cols,),
    )


COMBINE_COLUMNS = 512


def combine_kernel(
    combine_ref, place_ref, gate_ref, rider_ref, back_ref, shared_ref, router_ref, part_ref, dl_ref
):
    @pl.when(pl.program_id(0) == 0)
    def _():
        experts, rows = gate_ref.shape
        rider = rider_ref[...].astype(f32)
        value = rider[:, 0:1] + rider[:, 1:2]
        d_gate = place_ref[...].astype(f32) * value
        d_gate = jnp.sum(d_gate.reshape(experts, -1, rows), axis=1)
        gate = gate_ref[...]
        dl_ref[...] = gate * (d_gate - jnp.sum(gate * d_gate, axis=0, keepdims=True))

    total = dot_first(combine_ref[...], back_ref[...]) + shared_ref[...]
    total = total + dot_first(dl_ref[...].astype(bf16), router_ref[...])
    part_ref[...] = total.astype(bf16)


def combine_call(combine, place, gate, back, shared, router_t):
    slots, rows = combine.shape
    experts, width = router_t.shape
    cols = COMBINE_COLUMNS

    def whole(shape):
        return pl.BlockSpec(shape, lambda i: (0, 0))

    def tiled(height):
        return pl.BlockSpec((height, cols), lambda i: (0, i))

    return kernel_call(
        "combine_routes",
        combine_kernel,
        (combine, place, gate, back, back, shared, router_t),
        [
            whole((slots, rows)),
            whole((slots, rows)),
            whole((experts, rows)),
            pl.BlockSpec((slots, RIDER), lambda i: (0, width // RIDER)),
            tiled(slots),
            tiled(rows),
            tiled(experts),
        ],
        (struct((rows, width), bf16), struct((experts, rows), f32)),
        (tiled(rows), whole((experts, rows))),
        flops=2 * slots * rows * width,
        moved=8 * MIB,
        grid=(width // cols,),
    )


def mid_backward_kernel(
    idx, part_ref, g1, g2, g3, x1_ref, gain_ref, cot_ref, dx_ref, da_ref, gsum_ref
):
    d_two = own_sum(idx[4], part_ref, [g1, g2, g3])
    x1 = x1_ref[...]
    r2 = norm_rows(x1)
    gsum_ref[...] = jnp.broadcast_to(
        jnp.sum(d_two * x1 * r2, axis=0, keepdims=True), gsum_ref.shape
    )
    scaled = gain_ref[...] * d_two
    mean = jnp.mean(scaled * x1, axis=-1, keepdims=True)
    d_x1 = cot_ref[...].astype(f32) + r2 * scaled - x1 * (r2 * r2 * r2) * mean
    dx_ref[...] = d_x1
    da_ref[...] = d_x1.astype(bf16)


def first_backward_kernel(
    dkv_ref,
    turn_ref,
    wk_ref,
    wv_ref,
    dq_part_ref,
    tok_ref,
    dk_ref,
    dv_ref,
    part_ref,
    gsum_ref,
):
    total = jnp.sum(dkv_ref[...].astype(f32), axis=0)
    d_key = rotated(total[:, :HEAD_DIM], turn_ref[0], -turn_ref[1]).astype(bf16)
    d_value = total[:, HEAD_DIM:].astype(bf16)
    dk_ref[...] = d_key
    dv_ref[...] = d_value
    d_one = dq_part_ref[...] + dot_last(d_key, wk_ref[...]) + dot_last(d_value, wv_ref[...])
    part_ref[...] = d_one.astype(bf16)
    tok = tok_ref[...].astype(f32)
    gsum_ref[...] = jnp.broadcast_to(
        jnp.sum(d_one * tok * norm_rows(tok), axis=0, keepdims=True), gsum_ref.shape
    )


def input_rows_kernel(idx, part_ref, g1, g2, g3, tok_ref, gain_ref, dx_ref, out_ref):
    d_one = own_sum(idx[4], part_ref, [g1, g2, g3])
    tok = tok_ref[...].astype(f32)
    r1 = norm_rows(tok)
    scaled = gain_ref[...] * d_one
    mean = jnp.mean(scaled * tok, axis=-1, keepdims=True)
    out_ref[...] = (dx_ref[...] + r1 * scaled - tok * (r1 * r1 * r1) * mean).astype(bf16)


def output_rows_kernel(idx, part_ref, g1, g2, g3, x1_ref, out_ref):
    out_ref[...] = (x1_ref[...] + own_sum(idx[4], part_ref, [g1, g2, g3])).astype(bf16)


def assemble_kernel(idx, r0, r1, r2, r3, out_ref):
    put_rows(out_ref, idx[4], [r0, r1, r2, r3])


GRAD_ROWS = 256


def weight_grad_kernel(pairs, *refs):
    out_ref = refs[-1]
    at = 0
    cache = {}
    for left, rights in pairs:
        for right in rights:
            value = dot_first(refs[left][...], refs[right][...])
            columns = value.shape[1]
            key = (at, columns)
            cache[key] = value.astype(bf16)
            out_ref[:, at : at + columns] = cache[key]
            at += columns


def weight_grads(name, pairs):
    inputs, specs, plan, columns = [], [], [], 0
    width = pairs[0][0].shape[1]
    for left, rights in pairs:
        inputs.append(left)
        specs.append(pl.BlockSpec((left.shape[0], GRAD_ROWS), lambda i: (0, i)))
        left_at = len(inputs) - 1
        rights_at = []
        for right in rights:
            inputs.append(right)
            specs.append(pl.BlockSpec(right.shape, lambda i: (0, 0)))
            rights_at.append(len(inputs) - 1)
            columns += right.shape[1]
        plan.append((left_at, rights_at))
    return kernel_call(
        name,
        lambda *refs: weight_grad_kernel(plan, *refs),
        inputs,
        specs,
        struct((width, columns), bf16),
        pl.BlockSpec((GRAD_ROWS, columns), lambda i: (i, 0)),
        flops=2 * 128 * width * columns,
        moved=2 * width * columns,
        grid=(width // GRAD_ROWS,),
    )


def small_grad_kernel(h1_ref, dk_ref, dv_ref, h2_ref, dl_ref, gain_ref, pick_ref, out_ref):
    h1 = h1_ref[...]
    out_ref[:, 0:128] = dot_first(h1, dk_ref[...]).astype(bf16)
    out_ref[:, 128:256] = dot_first(h1, dv_ref[...]).astype(bf16)
    last = dot_first(h2_ref[...], dl_ref[...]) + dot_first(gain_ref[...], pick_ref[...])
    out_ref[:, 256:384] = last.astype(bf16)


def body(
    tokens,
    segments,
    routes,
    cotangent,
    attn_gain,
    w_query,
    key_weight,
    value_weight,
    w_out,
    ffn_gain,
    w_router,
    shared_gate,
    shared_up,
    shared_down,
    expert_gate,
    expert_up,
    expert_down,
):
    rows, width = tokens.shape
    experts = w_router.shape[1]
    top = routes.shape[1]
    slots = min(rows, rows * top // experts * 5 // 3)
    tp_count = lax.axis_size(TP)
    tp = lax.axis_index(TP)
    ep_count = lax.axis_size(EP)
    ep = lax.axis_index(EP)
    own = rows // tp_count
    quarter = width // tp_count
    qw = w_query.shape[1]
    heads = qw // HEAD_DIM
    all_tokens = ep_count * rows
    idx = jnp.stack(
        [lax.axis_index("x"), lax.axis_index("y"), lax.axis_index("core"), ep, tp]
    ).astype(jnp.int32)

    own_tokens = lax.dynamic_slice_in_dim(tokens, tp * own, own, axis=0)
    own_cot = lax.dynamic_slice_in_dim(cotangent, tp * own, own, axis=0)
    attn_row, ffn_row = attn_gain[None, :], ffn_gain[None, :]

    inverse = jnp.power(
        rope_base, -2.0 * jnp.arange(HEAD_DIM // 2, dtype=f32) / HEAD_DIM
    )
    angle = (ep * rows + jnp.arange(rows, dtype=jnp.int32)).astype(f32)[:, None] * inverse[None, :]
    cosine, sine = jnp.cos(angle), jnp.sin(angle)
    turn = jnp.stack(
        [jnp.concatenate([cosine, cosine], axis=1), jnp.concatenate([-sine, sine], axis=1)]
    )
    seg_rows = jnp.broadcast_to(segments[None, :], (8, rows))

    h1, payload = kernel_call(
        "key_value",
        key_value_kernel,
        (tokens, attn_row, key_weight, value_weight, turn, seg_rows),
        [VMEM] * 6,
        (struct((rows, width), bf16), struct((KV_ROWS, 2 * HEAD_DIM), bf16)),
        (VMEM, VMEM),
        flops=4 * rows * width * HEAD_DIM,
        moved=3 * MIB,
    )
    along_x = jnp.concatenate([payload] + [shift(payload, "x", k) for k in (1, 2, 3)], axis=0)
    along_y = [along_x] + [shift(along_x, "y", k) for k in (1, 2, 3)]
    across = [shift(block, "core", 1) for block in along_y]
    query = kernel_call(
        "query",
        query_kernel,
        (h1, w_query, turn),
        [VMEM] * 3,
        struct((rows, qw), bf16),
        VMEM,
        flops=2 * rows * width * qw,
        moved=5 * MIB,
    )
    below_two = jnp.sum((segments < 2).astype(jnp.int32))
    below_three = jnp.sum((segments < 3).astype(jnp.int32))
    start = jnp.where(
        segments == 0,
        0,
        jnp.where(
            segments == 1, -1, ep * rows + jnp.where(segments == 2, below_two, below_three)
        ),
    )
    start = jnp.broadcast_to(start.astype(jnp.int32)[None, :], (8, rows))

    mask_et = jnp.sum(
        (routes.T[:, None, :] == jnp.arange(experts, dtype=jnp.int32)[None, :, None]).astype(f32),
        axis=0,
    )
    before = jnp.arange(rows)[:, None] < jnp.arange(rows)[None, :]
    rank_et = dot_plain(mask_et.astype(bf16), before.astype(bf16))
    place = (rank_et[:, None, :] == jnp.arange(slots, dtype=f32)[None, :, None]) & (
        mask_et[:, None, :] > 0.5
    )
    place_low = place.astype(bf16).reshape(experts * slots, rows)
    own_columns = lax.dynamic_slice_in_dim(cotangent, tp * quarter, quarter, axis=1)
    g_out = dot_plain(place_low, own_columns).astype(bf16).reshape(experts, slots, quarter)

    core = lax.axis_index("core")
    by_core = h1.reshape(rows, ep_count // 2, 2, width // ep_count)
    h1_pair = [
        lax.dynamic_index_in_dim(by_core, which, axis=2, keepdims=False).reshape(rows, width // 2)
        for which in (core, 1 - core)
    ]
    h1_pair = jnp.concatenate([h1_pair[0], shift(h1_pair[1], "core", 1)], axis=0)

    heads_out, lse, kv, ahead, attn_part = kernel_call(
        "attn_forward",
        lambda *refs: attn_forward_kernel(heads, *refs),
        (idx, query, start, w_out, *along_y, *across),
        [SMEM] + [VMEM] * 11,
        (
            struct((rows, qw), bf16),
            struct((8, qw), f32),
            struct((all_tokens, 2 * HEAD_DIM), bf16),
            struct((8, 128), f32),
            struct((rows, width), bf16),
        ),
        (VMEM,) * 5,
        flops=4 * 2048 * 128 * qw,
        moved=12 * MIB,
    )
    g_out, attn_part = lax.optimization_barrier((g_out, attn_part))
    g_mine = exchange_ep(g_out).reshape(-1, quarter)

    x1, h2_own = kernel_call(
        "mid_norm",
        mid_norm_kernel,
        (idx, own_tokens, ffn_row, attn_part, *tp_pieces(attn_part, tp)),
        [SMEM] + [VMEM] * 6,
        (struct((own, width), f32), struct((own, width), bf16)),
        (VMEM, VMEM),
        moved=2 * MIB,
    )

    def fixed(shape):
        return pl.BlockSpec(shape, lambda i: (0, 0))

    h2, h2_out = kernel_call(
        "place_rows",
        place_kernel,
        (idx, h2_own, *tp_spread(h2_own), place_low),
        [SMEM]
        + [fixed((own, width))] * 4
        + [pl.BlockSpec((PLACE_ROWS, rows), lambda i: (i, 0))],
        (struct((rows, width), bf16), struct((experts * slots, width), bf16)),
        (fixed((rows, width)), pl.BlockSpec((PLACE_ROWS, width), lambda i: (i, 0))),
        flops=2 * experts * slots * rows * width,
        moved=8 * MIB,
        grid=(experts * slots // PLACE_ROWS,),
    )
    g_mine, h2, h2_out = lax.optimization_barrier((g_mine, h2, h2_out))
    g_in, u = cotangent_rows(idx, g_mine, expert_down[0])
    h2_in = exchange_ep(h2_out.reshape(experts, slots, width)).reshape(-1, width)

    logits_et = lax.dot_general(
        w_router, h2, (((0,), (1,)), ((), ())), preferred_element_type=f32
    )
    masked = jnp.where(mask_et > 0.5, logits_et, masked_score)
    expo = jnp.where(
        mask_et > 0.5, jnp.exp(masked - jnp.max(masked, axis=0, keepdims=True)), 0.0
    )
    gate_et = expo / jnp.sum(expo, axis=0, keepdims=True)
    placed_gate = jnp.where(place, gate_et[:, None, :], 0.0)
    combine = placed_gate.astype(bf16).reshape(experts * slots, rows)
    gate_slots = jnp.sum(placed_gate, axis=2)
    gate_slots = jnp.pad(gate_slots, ((0, 0), (0, 128 - slots)))
    gate_sent = jnp.broadcast_to(gate_slots[:, None, :], (experts, 8, 128))

    shared_act, d_shared_g, d_shared_u, shared_out, d_two_shared = shared_experts(
        h2, cotangent, shared_gate, shared_up, shared_down
    )
    shared_grads = weight_grads(
        "shared_grads", [(h2, [d_shared_g, d_shared_u]), (cotangent, [shared_act])]
    )
    w_both = jnp.concatenate([expert_gate[0], expert_up[0]], axis=1)
    (h2_in, shared_grads, shared_out, d_two_shared, w_both, u, h1_pair, combine, gate_sent) = (
        lax.optimization_barrier(
            (h2_in, shared_grads, shared_out, d_two_shared, w_both, u, h1_pair, combine, gate_sent)
        )
    )

    shared_sum = lax.psum_scatter(shared_grads, EP, scatter_dimension=0, tiled=True)

    gate_in = exchange_ep(gate_sent)[:, 0, :slots].reshape(-1, 1)
    act, d_both, d_in = expert_main(h2_in, u, w_both)
    ff = act.shape[1]
    d_in, gate_in = lax.optimization_barrier((d_in, gate_in))
    d_back = exchange_ep(d_in.reshape(ep_count, slots, width + RIDER))
    d_back = d_back.reshape(-1, width + RIDER)
    expert_down_grad = dot_first((act.astype(f32) * gate_in).astype(bf16), g_in)[None]
    d_both_gated = (d_both.astype(f32) * gate_in).astype(bf16)
    expert_gate_grad = dot_first(h2_in, d_both_gated[:, :ff])[None]
    expert_up_grad = dot_first(h2_in, d_both_gated[:, ff:])[None]
    act, expert_down_grad = lax.optimization_barrier((act, expert_down_grad))
    out_pieces = expert_out(idx, act, expert_down[0], tp_count)
    half = out_pieces.shape[1] // 2
    far_top = shift(out_pieces[2, :half], TP, 1)
    far_low = shift(out_pieces[2, half:], TP, -1)
    ahead_sum = jnp.concatenate([out_pieces[1, :half] + far_top, out_pieces[1, half:]], axis=0)
    behind_sum = jnp.concatenate([out_pieces[3, :half], out_pieces[3, half:] + far_low], axis=0)
    out_got = [shift(ahead_sum, TP, 1), shift(behind_sum, TP, -1)]
    d_back, out_pieces, expert_down_grad, expert_gate_grad, expert_up_grad = (
        lax.optimization_barrier(
            (d_back, out_pieces, expert_down_grad, expert_gate_grad, expert_up_grad)
        )
    )

    d_two_part, d_logits_et = combine_call(
        combine, place_low, gate_et, d_back, d_two_shared, w_router.T
    )
    out_own, out_got, d_two_part = lax.optimization_barrier((out_pieces[0], out_got, d_two_part))
    out_rows = out_own.astype(f32) + sum(piece.astype(f32) for piece in out_got)
    out_rows = out_rows.astype(bf16).reshape(ep_count, slots, quarter)
    out_back = exchange_ep(out_rows).reshape(-1, quarter)
    d_x1, d_attn_own, ffn_part = kernel_call(
        "mid_backward",
        mid_backward_kernel,
        (idx, d_two_part, *tp_pieces(d_two_part, tp), x1, ffn_row, own_cot),
        [SMEM] + [VMEM] * 7,
        (struct((own, width), f32), struct((own, width), bf16), struct((8, width), f32)),
        (VMEM,) * 3,
        moved=2 * MIB,
    )

    d_attn, d_query_raw, d_kv = kernel_call(
        "attn_backward",
        lambda *refs: attn_backward_kernel(heads, *refs),
        (idx, query, heads_out, lse, kv, ahead, start, turn, w_out)
        + (d_attn_own, *tp_spread(d_attn_own)),
        [SMEM] + [VMEM] * 12,
        (
            struct((rows, width), bf16),
            struct((rows, qw), bf16),
            struct((all_tokens, 2 * HEAD_DIM), bf16),
        ),
        (VMEM,) * 3,
        flops=10 * 2048 * 128 * qw,
        moved=12 * MIB,
    )
    out_grads = weight_grads("out_grads", [(d_attn, [heads_out])])
    d_kv, out_back, out_grads = lax.optimization_barrier((d_kv, out_back, out_grads))
    out_grads, shared_sum = lax.optimization_barrier((out_grads, shared_sum))
    out_sum = lax.psum_scatter(out_grads, EP, scatter_dimension=0, tiled=True)
    d_kv = exchange_ep(d_kv.reshape(ep_count, rows, 2 * HEAD_DIM))
    d_query_pair = jnp.concatenate([d_query_raw, shift(d_query_raw, "core", 1)], axis=0)
    query_grads = weight_grads("query_grads", [(h1_pair, [d_query_pair])])
    query_grads = query_grads.reshape(ep_count // 2, width // ep_count, qw)
    d_one_query = dot_last(d_query_raw, w_query)
    d_kv, d_one_query, query_grads = lax.optimization_barrier((d_kv, d_one_query, query_grads))
    d_key_raw, d_value, d_one_part, attn_part_sum = kernel_call(
        "first_backward",
        first_backward_kernel,
        (d_kv, turn, key_weight, value_weight, d_one_query, tokens),
        [VMEM] * 6,
        (
            struct((rows, HEAD_DIM), bf16),
            struct((rows, HEAD_DIM), bf16),
            struct((rows, width), bf16),
            struct((8, width), f32),
        ),
        (VMEM,) * 4,
        flops=4 * rows * width * HEAD_DIM,
        moved=8 * MIB,
    )
    query_grads, d_one_part = lax.optimization_barrier((query_grads, d_one_part))
    query_sum = lax.all_to_all(query_grads, CHIPS, 0, 0, tiled=True)
    query_sum = jnp.sum(query_sum.astype(f32), axis=0)
    input_own = kernel_call(
        "input_rows",
        input_rows_kernel,
        (idx, d_one_part, *tp_pieces(d_one_part, tp), own_tokens, attn_row, d_x1),
        [SMEM] + [VMEM] * 7,
        struct((own, width), bf16),
        VMEM,
        moved=2 * MIB,
    )
    input_grad = kernel_call(
        "input_all",
        assemble_kernel,
        (idx, input_own, *tp_spread(input_own)),
        [SMEM] + [VMEM] * 4,
        struct((rows, width), f32),
        VMEM,
        moved=2 * MIB,
    )

    d_logits_all = tp_sum_small(d_logits_et).T.astype(bf16)
    d_logits_all = jnp.pad(d_logits_all, ((0, 0), (0, 128 - experts)))
    attn_total = tp_sum_small(attn_part_sum[0:1])
    ffn_total = tp_sum_small(ffn_part[0:1])
    attn_high, ffn_high = attn_total.astype(bf16), ffn_total.astype(bf16)
    gains = jnp.concatenate(
        [
            attn_high,
            ffn_high,
            (attn_total - attn_high.astype(f32)).astype(bf16),
            (ffn_total - ffn_high.astype(f32)).astype(bf16),
            jnp.zeros((12, width), bf16),
        ],
        axis=0,
    )
    pick = (
        jnp.arange(16, dtype=jnp.int32)[:, None] + experts
        == jnp.arange(128, dtype=jnp.int32)[None, :]
    ).astype(bf16)

    def strip(height):
        return pl.BlockSpec((height, GRAD_ROWS), lambda i: (0, i))

    small = kernel_call(
        "small_grads",
        small_grad_kernel,
        (h1, d_key_raw, d_value, h2, d_logits_all, gains, pick),
        [strip(rows), fixed((rows, 128)), fixed((rows, 128)), strip(rows), fixed((rows, 128))]
        + [strip(16), fixed((16, 128))],
        struct((width, 384), bf16),
        pl.BlockSpec((GRAD_ROWS, 384), lambda i: (i, 0)),
        flops=2 * rows * width * 384,
        moved=3 * MIB,
        grid=(width // GRAD_ROWS,),
    )
    small, query_sum = lax.optimization_barrier((small, query_sum))
    small = exchange_ep(small.reshape(ep_count, width // ep_count, 384))
    small = jnp.sum(small.astype(f32), axis=0)
    gain_at = 2 * HEAD_DIM + experts

    routed = dot_first(combine, out_back)
    routed = lax.dynamic_update_slice_in_dim(
        jnp.zeros((rows, width), f32), routed, tp * quarter, axis=1
    )
    out_part = (shared_out + routed).astype(bf16)
    output_own = kernel_call(
        "output_rows",
        output_rows_kernel,
        (idx, out_part, *tp_pieces(out_part, tp), x1),
        [SMEM] + [VMEM] * 5,
        struct((own, width), bf16),
        VMEM,
        moved=2 * MIB,
    )
    output = kernel_call(
        "output_all",
        assemble_kernel,
        (idx, output_own, *tp_spread(output_own)),
        [SMEM] + [VMEM] * 4,
        struct((rows, width), bf16),
        VMEM,
        moved=2 * MIB,
    )

    sff = shared_act.shape[1]
    return (
        output,
        input_grad,
        small[:, gain_at] + small[:, gain_at + 2],
        query_sum,
        small[:, :HEAD_DIM],
        small[:, HEAD_DIM : 2 * HEAD_DIM],
        out_sum.astype(f32).T,
        small[:, gain_at + 1] + small[:, gain_at + 3],
        small[:, 2 * HEAD_DIM : gain_at],
        shared_sum[:, :sff].astype(f32),
        shared_sum[:, sff : 2 * sff].astype(f32),
        shared_sum[:, 2 * sff :].astype(f32).T,
        expert_gate_grad,
        expert_up_grad,
        expert_down_grad,
    )


def solution(mesh):
    ep_count, tp_count = mesh.shape["ep"], mesh.shape["tp"]
    side = math.isqrt(ep_count // 2)
    grid = Mesh(mesh.devices.reshape(side, side, 2, tp_count), EP + (TP,))
    return jax.shard_map(
        body,
        mesh=grid,
        in_specs=(
            P(EP, None),
            P(EP),
            P(EP, None),
            P(EP, None),
            P(),
            P(None, TP),
            P(None, TP),
            P(None, TP),
            P(TP, None),
            P(),
            P(),
            P(None, TP),
            P(None, TP),
            P(TP, None),
            P(EP, None, TP),
            P(EP, None, TP),
            P(EP, TP, None),
        ),
        out_specs=(
            P(EP, None),
            P(EP, None),
            P(EP),
            P(EP, TP),
            P(EP, TP),
            P(EP, TP),
            P(TP, EP),
            P(EP),
            P(EP, None),
            P(EP, TP),
            P(EP, TP),
            P(TP, EP),
            P(EP, None, TP),
            P(EP, None, TP),
            P(EP, TP, None),
        ),
        check_vma=False,
    )
```

```python
import math

import jax
import jax.numpy as jnp
from jax import lax
from jax.experimental import pallas as pl
from jax.experimental.pallas import tpu as pltpu
from jax.sharding import Mesh
from jax.sharding import PartitionSpec as P

HEAD_DIM = 128
EP = ("x", "y", "core")
TP = "tp"

eps_norm = 1e-05
rope_base = 500000.0
masked_score = -1e30

bf16 = jnp.bfloat16
f32 = jnp.float32

VMEM = pl.BlockSpec(memory_space=pltpu.VMEM)
SMEM = pl.BlockSpec(memory_space=pltpu.SMEM)
MIB = 1024 * 1024


def dot_plain(left, right):
    return jnp.dot(left, right, preferred_element_type=f32)


def dot_last(left, right):
    dims = (((left.ndim - 1,), (right.ndim - 1,)), ((), ()))
    return lax.dot_general(left, right, dims, preferred_element_type=f32)


def dot_first(left, right):
    return lax.dot_general(left, right, (((0,), (0,)), ((), ())), preferred_element_type=f32)


def struct(shape, dtype):
    return jax.ShapeDtypeStruct(shape, dtype)


def kernel_call(name, kernel, inputs, in_specs, out_shape, out_specs, flops=0, moved=0, **more):
    return pl.pallas_call(
        kernel,
        out_shape=out_shape,
        in_specs=in_specs,
        out_specs=out_specs,
        compiler_params=pltpu.CompilerParams(vmem_limit_bytes=48 * MIB),
        cost_estimate=pl.CostEstimate(flops=flops, bytes_accessed=moved, transcendentals=0),
        name=name,
        **more,
    )(*inputs)


def shift(values, axis, step):
    size = lax.axis_size(axis)
    return lax.ppermute(values, axis, [(i, (i + step) % size) for i in range(size)])


def exchange_ep(values):
    return lax.all_to_all(values, EP, 0, 0, tiled=True)


def tp_pieces(part, tp):
    count = lax.axis_size(TP)
    own = part.shape[0] // count
    got = []
    for step in range(1, count):
        piece = lax.dynamic_slice_in_dim(part, (tp + step) % count * own, own, axis=0)
        got.append(shift(piece, TP, step))
    return got


def tp_spread(rows):
    return [shift(rows, TP, step) for step in range(1, lax.axis_size(TP))]


def tp_sum_small(value):
    total = value
    for step in range(1, lax.axis_size(TP)):
        total = total + shift(value, TP, step)
    return total


def tp_neighbours(mine):
    half = mine.shape[0] // 2
    top, low = mine[:half], mine[half:]
    before_top, after_low = shift(top, TP, 1), shift(low, TP, -1)
    before_low, after_top = shift(low, TP, 1), shift(top, TP, -1)
    return [mine, before_top, before_low, after_top, after_low]


def tp_quarters(near):
    return [*near, shift(near[1], TP, 1), shift(near[4], TP, -1)]


def tp_sum_quarters(first, second_top, second_low, third_top, third_low, fourth_top, fourth_low):
    far_top, far_low = shift(third_top, TP, 1), shift(third_low, TP, -1)
    from_before_low = shift(second_low, TP, 1)
    from_after_top = shift(fourth_top, TP, -1)
    from_before_top = shift(second_top + far_top, TP, 1)
    from_after_low = shift(fourth_low + far_low, TP, -1)
    return [first, from_before_top, from_before_low, from_after_top, from_after_low]


def put_rows(target_ref, tp, pieces):
    own = pieces[0].shape[0]
    for step, piece in enumerate(pieces):
        at = ((tp - step) & 3) * own
        target_ref[pl.ds(pl.multiple_of(at, own), own), :] = piece[...].astype(target_ref.dtype)


def own_sum(tp, part_ref, got):
    own = got[0].shape[0]
    total = part_ref[pl.ds(pl.multiple_of(tp * own, own), own), :].astype(f32)
    for piece in got:
        total = total + piece[...].astype(f32)
    return total


KV_ROWS = 144


def rotated(values, cosine, sine):
    return values * cosine + pltpu.roll(values, HEAD_DIM // 2, 1) * sine


def norm_rows(values):
    return lax.rsqrt(jnp.mean(values * values, axis=-1, keepdims=True) + eps_norm)


def key_value_kernel(
    tok_ref, gain_ref, wk_ref, wv_ref, turn_ref, seg_ref, route_ref, h1_ref, kv_ref
):
    tok = tok_ref[...].astype(f32)
    h1 = (tok * norm_rows(tok) * gain_ref[...]).astype(bf16)
    h1_ref[...] = h1
    rows = tok.shape[0]
    key = rotated(dot_plain(h1, wk_ref[...]), turn_ref[0], turn_ref[1])
    kv_ref[0:rows, 0:HEAD_DIM] = key.astype(bf16)
    kv_ref[0:rows, HEAD_DIM:] = dot_plain(h1, wv_ref[...]).astype(bf16)
    zeros = jnp.sum((seg_ref[0:1, :] == 0).astype(f32), axis=1, keepdims=True)
    line = lax.broadcasted_iota(jnp.int32, route_ref.shape, 0)
    notes = jnp.where(line == 0, zeros, route_ref[...]).astype(bf16)
    kv_ref[rows:, 0:HEAD_DIM] = notes
    kv_ref[rows:, HEAD_DIM:] = notes


def query_kernel(h1_ref, wq_ref, turn_ref, q_ref):
    raw = dot_plain(h1_ref[...], wq_ref[...])
    for at in range(0, raw.shape[1], HEAD_DIM):
        head = raw[:, at : at + HEAD_DIM]
        q_ref[:, at : at + HEAD_DIM] = rotated(head, turn_ref[0], turn_ref[1]).astype(bf16)


CHUNK = 1024


def first_allowed(notes_ref, start_ref):
    start = start_ref[0:1, :]
    ahead = notes_ref[0:16, :].astype(f32)[0:1, :]
    return jnp.where(start < 0, ahead.astype(jnp.int32), start)


def chunk_mask(chunk, start, query_ids, heads):
    key_ids = chunk * CHUNK + lax.broadcasted_iota(jnp.int32, (CHUNK, 128), 0)
    mask = (key_ids >= start) & (key_ids <= query_ids)
    return jnp.concatenate([mask] * heads, axis=1)


def stack_heads(values, heads):
    return jnp.concatenate([values[:, h * 128 : (h + 1) * 128] for h in range(heads)], axis=0)


def attn_forward_kernel(heads, idx, q_ref, start_ref, wo_ref, *refs):
    sources, (o_ref, lse_ref, kv_ref, notes_ref, part_ref) = refs[:8], refs[8:]
    scale = HEAD_DIM ** (-0.5)
    wide = heads * 128
    x, y, core, ep = idx[0], idx[1], idx[2], idx[3]
    for near in range(2):
        for dy in range(4):
            source = sources[near * 4 + dy]
            for dx in range(4):
                block = ((x - dx) & 3) * 8 + ((y - dy) & 3) * 2 + (core ^ near)
                at = pl.ds(pl.multiple_of(block * 128, 128), 128)
                kv_ref[at, :] = source[dx * KV_ROWS : dx * KV_ROWS + 128, :]

                note_at = pl.ds(pl.multiple_of(block * 16, 16), 16)
                notes_ref[note_at, :] = source[dx * KV_ROWS + 128 : (dx + 1) * KV_ROWS, 0:128]

    queries = stack_heads(q_ref[...], heads)
    start = first_allowed(notes_ref, start_ref)
    query_ids = ep * 128 + lax.broadcasted_iota(jnp.int32, (1, 128), 1)

    def step(chunk, carry):
        top, total, acc = carry
        at = pl.ds(pl.multiple_of(chunk * CHUNK, CHUNK), CHUNK)
        keys, values = kv_ref[at, 0:128], kv_ref[at, 128:256]
        scores = dot_last(keys, queries) * scale
        scores = jnp.where(chunk_mask(chunk, start, query_ids, heads), scores, masked_score)
        new_top = jnp.maximum(top, jnp.max(scores, axis=0, keepdims=True))
        prob = jnp.exp(scores - new_top)
        fade = jnp.exp(top - new_top)
        total = total * fade + jnp.sum(prob, axis=0, keepdims=True)
        acc = acc * fade + dot_first(values, prob.astype(bf16))
        return new_top, total, acc

    chunks = (ep * 128 + 127) // CHUNK + 1
    top, total, acc = lax.fori_loop(
        0,
        chunks,
        step,
        (
            jnp.full((1, wide), masked_score, f32),
            jnp.zeros((1, wide), f32),
            jnp.zeros((HEAD_DIM, wide), f32),
        ),
    )
    out = acc / total
    out = jnp.concatenate(
        [out[:, h * 128 : (h + 1) * 128].T.astype(bf16) for h in range(heads)], axis=1
    )
    o_ref[...] = out
    lse_ref[...] = jnp.broadcast_to(top + jnp.log(total), lse_ref.shape)
    part_ref[...] = dot_plain(out, wo_ref[...]).astype(bf16)


def attn_backward_kernel(
    heads,
    idx,
    q_ref,
    o_ref,
    lse_ref,
    kv_ref,
    notes_ref,
    start_ref,
    turn_ref,
    wo_ref,
    r0,
    r1,
    r2,
    r3,
    da_ref,
    dq_ref,
    dkv_ref,
):
    scale = HEAD_DIM ** (-0.5)
    wide = heads * 128
    ep, tp = idx[3], idx[4]
    put_rows(da_ref, tp, [r0, r1, r2, r3])
    d_heads = dot_last(da_ref[...], wo_ref[...]).astype(bf16)
    queries = stack_heads(q_ref[...], heads)
    douts = stack_heads(d_heads, heads)
    outs = stack_heads(o_ref[...], heads)
    lse = lse_ref[0:1, :]
    product = douts.astype(f32) * outs.astype(f32)
    high = product.astype(bf16)
    low = (product - high.astype(f32)).astype(bf16)
    ones = jnp.ones((16, HEAD_DIM), bf16)
    delta = (dot_last(ones, high) + dot_last(ones, low))[0:1, :]
    start = first_allowed(notes_ref, start_ref)
    query_ids = ep * 128 + lax.broadcasted_iota(jnp.int32, (1, 128), 1)
    dkv_ref[...] = jnp.zeros_like(dkv_ref)

    def step(chunk, dq):
        at = pl.ds(pl.multiple_of(chunk * CHUNK, CHUNK), CHUNK)
        keys, values = kv_ref[at, 0:128], kv_ref[at, 128:256]
        scores = dot_last(keys, queries) * scale
        mask = chunk_mask(chunk, start, query_ids, heads)
        prob = jnp.where(mask, jnp.exp(scores - lse), 0.0)
        dprob = dot_last(values, douts)
        dscore = (prob * (dprob - delta) * scale).astype(bf16)
        dkv_ref[at, 0:128] = dot_plain(dscore, queries).astype(bf16)
        dkv_ref[at, 128:256] = dot_plain(prob.astype(bf16), douts).astype(bf16)
        return dq + dot_first(keys, dscore)

    chunks = (ep * 128 + 127) // CHUNK + 1
    dq = lax.fori_loop(0, chunks, step, jnp.zeros((HEAD_DIM, wide), f32))
    for h in range(heads):
        at = slice(h * 128, (h + 1) * 128)
        dq_ref[:, at] = rotated(dq[:, at].T, turn_ref[0], -turn_ref[1]).astype(bf16)


def mid_norm_kernel(idx, tok_ref, gain_ref, part_ref, g1, g2, g3, x1_ref, h2_ref):
    x1 = tok_ref[...].astype(f32) + own_sum(idx[4], part_ref, [g1, g2, g3])
    x1_ref[...] = x1
    h2_ref[...] = (x1 * norm_rows(x1) * gain_ref[...]).astype(bf16)


EXPERT_ROWS = 640
RIDER = 128


def put_quarters(target_ref, tp, own_ref, pieces):
    quarter = own_ref.shape[1]

    def put(owner, ref):
        at = (owner & 3) * quarter
        target_ref[:, pl.ds(pl.multiple_of(at, 128), quarter)] = ref[...]

    put(tp, own_ref)
    before_top, before_low, after_top, after_low, far_top, far_low = pieces

    @pl.when(pl.program_id(0) == 0)
    def _():
        put(tp + 3, before_top)
        put(tp + 1, after_top)
        put(tp + 2, far_top)

    @pl.when(pl.program_id(0) == 1)
    def _():
        put(tp + 3, before_low)
        put(tp + 1, after_low)
        put(tp + 2, far_low)


def rowed(columns):
    return pl.BlockSpec((EXPERT_ROWS, columns), lambda i: (i, 0))


def fixed(shape):
    return pl.BlockSpec(shape, lambda i: (0, 0))


def cotangent_rows_kernel(idx, own_ref, *refs):
    pieces, (down_ref, g_ref, u_ref) = refs[:6], refs[6:]
    put_quarters(g_ref, idx[4], own_ref, pieces)
    u_ref[...] = dot_last(g_ref[...], down_ref[...])


def cotangent_rows(idx, quarters, down):
    slots, quarter = quarters[0].shape
    ff, width = down.shape
    return kernel_call(
        "cotangent_rows",
        cotangent_rows_kernel,
        (idx, *quarters, down),
        [SMEM, rowed(quarter)] + [fixed((EXPERT_ROWS, quarter))] * 6 + [fixed((ff, width))],
        (struct((slots, width), bf16), struct((slots, ff), f32)),
        (rowed(width), rowed(ff)),
        flops=2 * slots * width * ff,
        moved=16 * MIB,
        grid=(slots // EXPERT_ROWS,),
    )


SOURCES = 8


def pick_rows(places, hidden_ref, out_ref, slots):
    rows = places.shape[1]
    slot = lax.broadcasted_iota(jnp.int32, (2 * slots, 2 * rows), 0)
    column = lax.broadcasted_iota(jnp.int32, (2 * slots, 2 * rows), 1)
    second = slot >= slots
    same = second == (column >= rows)
    wanted = jnp.where(second, slot - slots, slot).astype(f32)
    for pair in range(places.shape[0] // 2):
        at = 2 * pair
        line = jnp.concatenate([places[at : at + 1], places[at + 1 : at + 2]], axis=1)
        hit = jnp.where(same & (line == wanted), 1.0, 0.0).astype(bf16)
        tokens = hidden_ref[2 * pair * rows : 2 * (pair + 1) * rows, :]
        out_ref[2 * pair * slots : 2 * (pair + 1) * slots, :] = dot_plain(hit, tokens).astype(bf16)


def expert_kernel(slots, hidden_ref, places_ref, u_ref, gate_in_ref, w_ref, turned_ref, *outs):
    x_ref, ea_ref, ga_ref, dgu_ref, rider_ref, first_ref = outs[:6]
    halves = ((outs[6], outs[7]), (outs[8], outs[9]), (outs[10], outs[11]))
    ff = ea_ref.shape[1]
    rows = x_ref.shape[0]
    quarter = first_ref.shape[1]
    low = pl.program_id(0) >= pl.num_programs(0) // 2
    pick_rows(places_ref[...], hidden_ref, x_ref, slots)
    both = dot_plain(x_ref[...], w_ref[...])
    gate, up = both[:, :ff], both[:, ff:]
    sig = 1.0 / (1.0 + jnp.exp(-gate))
    silu = gate * sig
    act = silu * up
    ea_ref[...] = act.astype(bf16)
    route_gate = gate_in_ref[...]
    ga_ref[...] = (act * route_gate).astype(bf16)
    plain = u_ref[...]
    dgates = jnp.sum(plain * act, axis=1, keepdims=True)
    dact = plain * route_gate
    dup = dact * silu
    dgate = dact * up * (sig * (1.0 + gate * (1.0 - sig)))
    dboth = jnp.concatenate([dgate, dup], axis=1).astype(bf16)
    dgu_ref[...] = dboth
    high = dgates.astype(bf16).astype(f32)
    lane = lax.broadcasted_iota(jnp.int32, (rows, RIDER), 1)
    rider = jnp.where(lane == 0, high, jnp.where(lane == 1, dgates - high, 0.0))
    rider_ref[...] = rider.astype(bf16)
    d_in = dot_last(dboth, turned_ref[...]).astype(bf16)
    first_ref[...] = d_in[:, :quarter]

    @pl.when(jnp.logical_not(low))
    def _():
        for ahead in range(3):
            halves[ahead][0][...] = d_in[:, (ahead + 1) * quarter : (ahead + 2) * quarter]

    @pl.when(low)
    def _():
        for ahead in range(3):
            halves[ahead][1][...] = d_in[:, (ahead + 1) * quarter : (ahead + 2) * quarter]


def expert_main(hidden, places, u, gate_in, w_both, w_turned, quarter):
    sources, rows = places.shape
    slots_all, ff = u.shape
    slots = slots_all // sources
    width = hidden.shape[1]
    block = SOURCES * slots
    steps = sources // SOURCES
    half = struct((slots_all // 2, quarter), bf16)

    def lined(columns):
        return pl.BlockSpec((block, columns), lambda i: (i, 0))

    top_half = pl.BlockSpec((block, quarter), lambda i: (jnp.minimum(i, steps // 2 - 1), 0))
    low_half = pl.BlockSpec((block, quarter), lambda i: (jnp.maximum(i - steps // 2, 0), 0))
    return kernel_call(
        "expert_main",
        lambda *refs: expert_kernel(slots, *refs),
        (hidden, places, u, gate_in, w_both, w_turned),
        [
            pl.BlockSpec((SOURCES * rows, width), lambda i: (i, 0)),
            pl.BlockSpec((SOURCES, rows), lambda i: (i, 0)),
            lined(ff),
            lined(1),
            fixed((width, 2 * ff)),
            fixed((width, 2 * ff)),
        ],
        (
            struct((slots_all, width), bf16),
            struct((slots_all, ff), bf16),
            struct((slots_all, ff), bf16),
            struct((slots_all, 2 * ff), bf16),
            struct((slots_all, RIDER), bf16),
            struct((slots_all, quarter), bf16),
        )
        + (half,) * 6,
        (lined(width), lined(ff), lined(ff), lined(2 * ff), lined(RIDER), lined(quarter))
        + (top_half, low_half) * 3,
        flops=8 * slots_all * width * ff,
        moved=50 * MIB,
        grid=(steps,),
    )


def quarter_sum_kernel(first_ref, bt_ref, bl_ref, at_ref, al_ref, rider_ref, out_ref):
    quarter = first_ref.shape[1]
    out_ref[:, quarter:] = rider_ref[...]
    first = first_ref[...].astype(f32)

    @pl.when(pl.program_id(0) == 0)
    def _():
        total = first + bt_ref[...].astype(f32) + at_ref[...].astype(f32)
        out_ref[:, :quarter] = total.astype(bf16)

    @pl.when(pl.program_id(0) == 1)
    def _():
        total = first + bl_ref[...].astype(f32) + al_ref[...].astype(f32)
        out_ref[:, :quarter] = total.astype(bf16)


def quarter_sum(parts, rider):
    slots, quarter = parts[0].shape
    half = (EXPERT_ROWS, quarter)
    return kernel_call(
        "quarter_sum",
        quarter_sum_kernel,
        (*parts, rider),
        [rowed(quarter)] + [fixed(half)] * 4 + [rowed(RIDER)],
        struct((slots, quarter + RIDER), bf16),
        rowed(quarter + RIDER),
        moved=8 * MIB,
        grid=(slots // EXPERT_ROWS,),
    )


OUT_COLUMNS = 512
OUT_FIRST = 3


def expert_out_kernel(act_ref, down_ref, *out_refs):
    at = 0
    for out_ref in out_refs:
        end = at + out_ref.shape[1]
        out_ref[...] = dot_plain(act_ref[...], down_ref[:, at:end]).astype(bf16)
        at = end


def expert_out(act, down):
    slots, ff = act.shape
    width = down.shape[1]
    parts = [OUT_FIRST * OUT_COLUMNS, width - OUT_FIRST * OUT_COLUMNS]
    return kernel_call(
        "expert_out",
        expert_out_kernel,
        (act, down),
        [rowed(ff), fixed((ff, width))],
        tuple(struct((slots, part), bf16) for part in parts),
        tuple(rowed(part) for part in parts),
        flops=2 * slots * ff * width,
        moved=9 * MIB,
        grid=(slots // EXPERT_ROWS,),
    )


def output_part_kernel(combine_ref, one_ref, two_ref, shared_ref, part_ref):
    here = pl.program_id(0)

    def write(ref):
        part_ref[...] = (dot_first(combine_ref[...], ref[...]) + shared_ref[...]).astype(bf16)

    pl.when(here < OUT_FIRST)(lambda: write(one_ref))
    pl.when(here >= OUT_FIRST)(lambda: write(two_ref))


def output_part(combine, one, two, shared):
    slots, rows = combine.shape
    width = shared.shape[1]
    cols = OUT_COLUMNS
    return kernel_call(
        "output_part",
        output_part_kernel,
        (combine, one, two, shared),
        [
            fixed((slots, rows)),
            pl.BlockSpec((slots, cols), lambda i: (0, jnp.minimum(i, OUT_FIRST - 1))),
            pl.BlockSpec((slots, cols), lambda i: (0, jnp.maximum(i - OUT_FIRST, 0))),
            pl.BlockSpec((rows, cols), lambda i: (0, i)),
        ],
        struct((rows, width), bf16),
        pl.BlockSpec((rows, cols), lambda i: (0, i)),
        flops=2 * slots * rows * width,
        moved=8 * MIB,
        grid=(width // cols,),
    )


SHARED_COLUMNS = 256


def shared_kernel(
    h2_ref, cot_ref, gate_ref, up_ref, down_ref, act_ref, dg_ref, du_ref, out_ref, dh_ref
):
    gate = dot_plain(h2_ref[...], gate_ref[...])
    up = dot_plain(h2_ref[...], up_ref[...])
    dact = dot_last(cot_ref[...], down_ref[...])
    sig = 1.0 / (1.0 + jnp.exp(-gate))
    silu = gate * sig
    act = (silu * up).astype(bf16)
    dgate = (dact * up * (sig * (1.0 + gate * (1.0 - sig)))).astype(bf16)
    dup = (dact * silu).astype(bf16)
    act_ref[...] = act
    dg_ref[...] = dgate
    du_ref[...] = dup
    out = dot_plain(act, down_ref[...])
    dh = dot_last(dgate, gate_ref[...]) + dot_last(dup, up_ref[...])
    first = pl.program_id(0) == 0

    @pl.when(first)
    def _():
        out_ref[...] = out
        dh_ref[...] = dh

    @pl.when(jnp.logical_not(first))
    def _():
        out_ref[...] += out
        dh_ref[...] += dh


def shared_experts(h2, cotangent, gate, up, down):
    rows, width = h2.shape
    hidden = gate.shape[1]
    cols = SHARED_COLUMNS
    whole = pl.BlockSpec((rows, width), lambda i: (0, 0))
    column = pl.BlockSpec((width, cols), lambda i: (0, i))
    hid = pl.BlockSpec((rows, cols), lambda i: (0, i))
    return kernel_call(
        "shared_experts",
        shared_kernel,
        (h2, cotangent, gate, up, down),
        [whole, whole, column, column, pl.BlockSpec((cols, width), lambda i: (i, 0))],
        (struct((rows, hidden), bf16),) * 3 + (struct((rows, width), f32),) * 2,
        (hid, hid, hid, whole, whole),
        flops=14 * rows * width * hidden,
        moved=16 * MIB,
        grid=(hidden // cols,),
    )


def combine_kernel(idx, place_ref, gate_ref, back_ref, shared_ref, router_ref, part_ref, dl_ref):
    experts, rows = gate_ref.shape
    quarter = back_ref.shape[1] - RIDER
    rider = back_ref[:, quarter:].astype(f32)
    d_gate = place_ref[...].astype(f32) * (rider[:, 0:1] + rider[:, 1:2])
    d_gate = jnp.sum(d_gate.reshape(experts, -1, rows), axis=1)
    gate = gate_ref[...]
    d_logits = gate * (d_gate - jnp.sum(gate * d_gate, axis=0, keepdims=True))
    dl_ref[...] = d_logits
    low = d_logits.astype(bf16)
    part_ref[...] = (shared_ref[...] + dot_first(low, router_ref[...])).astype(bf16)
    columns = pl.ds(pl.multiple_of(idx[4] * quarter, 128), quarter)
    total = dot_first(place_ref[...], back_ref[:, :quarter])
    total = total + shared_ref[:, columns] + dot_first(low, router_ref[:, columns])
    part_ref[:, columns] = total.astype(bf16)


def combine_call(idx, place, gate, back, shared, router_t):
    slots, rows = place.shape
    experts, width = router_t.shape
    return kernel_call(
        "combine_routes",
        combine_kernel,
        (idx, place, gate, back, shared, router_t),
        [SMEM] + [VMEM] * 5,
        (struct((rows, width), bf16), struct((experts, rows), f32)),
        (VMEM, VMEM),
        flops=2 * slots * rows * width // 4,
        moved=4 * MIB,
    )


def mid_backward_kernel(
    idx, part_ref, g1, g2, g3, x1_ref, gain_ref, cot_ref, dx_ref, da_ref, gsum_ref
):
    d_two = own_sum(idx[4], part_ref, [g1, g2, g3])
    x1 = x1_ref[...]
    r2 = norm_rows(x1)
    gsum_ref[...] = jnp.broadcast_to(
        jnp.sum(d_two * x1 * r2, axis=0, keepdims=True), gsum_ref.shape
    )
    scaled = gain_ref[...] * d_two
    mean = jnp.mean(scaled * x1, axis=-1, keepdims=True)
    d_x1 = cot_ref[...].astype(f32) + r2 * scaled - x1 * (r2 * r2 * r2) * mean
    dx_ref[...] = d_x1
    da_ref[...] = d_x1.astype(bf16)


def first_backward_kernel(
    dkv_ref,
    turn_ref,
    wk_ref,
    wv_ref,
    dq_part_ref,
    tok_ref,
    dk_ref,
    dv_ref,
    part_ref,
    gsum_ref,
):
    total = jnp.sum(dkv_ref[...].astype(f32), axis=0)
    d_key = rotated(total[:, :HEAD_DIM], turn_ref[0], -turn_ref[1]).astype(bf16)
    d_value = total[:, HEAD_DIM:].astype(bf16)
    dk_ref[...] = d_key
    dv_ref[...] = d_value
    d_one = dq_part_ref[...] + dot_last(d_key, wk_ref[...]) + dot_last(d_value, wv_ref[...])
    part_ref[...] = d_one.astype(bf16)
    tok = tok_ref[...].astype(f32)
    gsum_ref[...] = jnp.broadcast_to(
        jnp.sum(d_one * tok * norm_rows(tok), axis=0, keepdims=True), gsum_ref.shape
    )


def input_rows_kernel(idx, part_ref, g1, g2, g3, tok_ref, gain_ref, dx_ref, out_ref):
    d_one = own_sum(idx[4], part_ref, [g1, g2, g3])
    tok = tok_ref[...].astype(f32)
    r1 = norm_rows(tok)
    scaled = gain_ref[...] * d_one
    mean = jnp.mean(scaled * tok, axis=-1, keepdims=True)
    out_ref[...] = (dx_ref[...] + r1 * scaled - tok * (r1 * r1 * r1) * mean).astype(bf16)


def output_rows_kernel(idx, part_ref, g1, g2, g3, x1_ref, out_ref):
    out_ref[...] = (x1_ref[...] + own_sum(idx[4], part_ref, [g1, g2, g3])).astype(bf16)


def assemble_kernel(idx, r0, r1, r2, r3, out_ref):
    put_rows(out_ref, idx[4], [r0, r1, r2, r3])


GRAD_ROWS = 256


def weight_grad_kernel(pairs, *refs):
    out_ref = refs[-1]
    at = 0
    cache = {}
    for left, rights in pairs:
        for right in rights:
            value = dot_first(refs[left][...], refs[right][...])
            columns = value.shape[1]
            key = (at, columns)
            cache[key] = value.astype(bf16)
            out_ref[:, at : at + columns] = cache[key]
            at += columns


def weight_grads(name, pairs):
    inputs, specs, plan, columns = [], [], [], 0
    width = pairs[0][0].shape[1]
    for left, rights in pairs:
        inputs.append(left)
        specs.append(pl.BlockSpec((left.shape[0], GRAD_ROWS), lambda i: (0, i)))
        left_at = len(inputs) - 1
        rights_at = []
        for right in rights:
            inputs.append(right)
            specs.append(pl.BlockSpec(right.shape, lambda i: (0, 0)))
            rights_at.append(len(inputs) - 1)
            columns += right.shape[1]
        plan.append((left_at, rights_at))
    return kernel_call(
        name,
        lambda *refs: weight_grad_kernel(plan, *refs),
        inputs,
        specs,
        struct((width, columns), bf16),
        pl.BlockSpec((GRAD_ROWS, columns), lambda i: (i, 0)),
        flops=2 * 128 * width * columns,
        moved=2 * width * columns,
        grid=(width // GRAD_ROWS,),
    )


def small_grad_kernel(h1_ref, dk_ref, dv_ref, h2_ref, dl_ref, gain_ref, pick_ref, out_ref):
    h1 = h1_ref[...]
    out_ref[:, 0:128] = dot_first(h1, dk_ref[...]).astype(bf16)
    out_ref[:, 128:256] = dot_first(h1, dv_ref[...]).astype(bf16)
    last = dot_first(h2_ref[...], dl_ref[...]) + dot_first(gain_ref[...], pick_ref[...])
    out_ref[:, 256:384] = last.astype(bf16)


def body(
    tokens,
    segments,
    routes,
    cotangent,
    attn_gain,
    w_query,
    key_weight,
    value_weight,
    w_out,
    ffn_gain,
    w_router,
    shared_gate,
    shared_up,
    shared_down,
    expert_gate,
    expert_up,
    expert_down,
):
    rows, width = tokens.shape
    experts = w_router.shape[1]
    top = routes.shape[1]
    slots = min(rows, rows * top // experts * 5 // 3)
    tp_count = lax.axis_size(TP)
    tp = lax.axis_index(TP)
    ep_count = lax.axis_size(EP)
    ep = lax.axis_index(EP)
    own = rows // tp_count
    quarter = width // tp_count
    qw = w_query.shape[1]
    heads = qw // HEAD_DIM
    all_tokens = ep_count * rows
    idx = jnp.stack(
        [lax.axis_index("x"), lax.axis_index("y"), lax.axis_index("core"), ep, tp]
    ).astype(jnp.int32)

    own_tokens = lax.dynamic_slice_in_dim(tokens, tp * own, own, axis=0)
    own_cot = lax.dynamic_slice_in_dim(cotangent, tp * own, own, axis=0)
    attn_row, ffn_row = attn_gain[None, :], ffn_gain[None, :]

    inverse = jnp.power(
        rope_base, -2.0 * jnp.arange(HEAD_DIM // 2, dtype=f32) / HEAD_DIM
    )
    angle = (ep * rows + jnp.arange(rows, dtype=jnp.int32)).astype(f32)[:, None] * inverse[None, :]
    cosine, sine = jnp.cos(angle), jnp.sin(angle)
    turn = jnp.stack(
        [jnp.concatenate([cosine, cosine], axis=1), jnp.concatenate([-sine, sine], axis=1)]
    )
    seg_rows = jnp.broadcast_to(segments[None, :], (8, rows))
    route_rows = jnp.pad(routes.T.astype(f32), ((1, 16 - 1 - top), (0, 0)))

    h1, payload = kernel_call(
        "key_value",
        key_value_kernel,
        (tokens, attn_row, key_weight, value_weight, turn, seg_rows, route_rows),
        [VMEM] * 7,
        (struct((rows, width), bf16), struct((KV_ROWS, 2 * HEAD_DIM), bf16)),
        (VMEM, VMEM),
        flops=4 * rows * width * HEAD_DIM,
        moved=3 * MIB,
    )
    along_x = jnp.concatenate([payload] + [shift(payload, "x", k) for k in (1, 2, 3)], axis=0)
    along_y = [along_x] + [shift(along_x, "y", k) for k in (1, 2, 3)]
    across = [shift(block, "core", 1) for block in along_y]
    query = kernel_call(
        "query",
        query_kernel,
        (h1, w_query, turn),
        [VMEM] * 3,
        struct((rows, qw), bf16),
        VMEM,
        flops=2 * rows * width * qw,
        moved=5 * MIB,
    )
    below_two = jnp.sum((segments < 2).astype(jnp.int32))
    below_three = jnp.sum((segments < 3).astype(jnp.int32))
    start = jnp.where(
        segments == 0,
        0,
        jnp.where(
            segments == 1, -1, ep * rows + jnp.where(segments == 2, below_two, below_three)
        ),
    )
    start = jnp.broadcast_to(start.astype(jnp.int32)[None, :], (8, rows))

    mask_et = jnp.sum(
        (routes.T[:, None, :] == jnp.arange(experts, dtype=jnp.int32)[None, :, None]).astype(f32),
        axis=0,
    )
    before = jnp.arange(rows)[:, None] < jnp.arange(rows)[None, :]
    rank_et = dot_plain(mask_et.astype(bf16), before.astype(bf16))
    place = (rank_et[:, None, :] == jnp.arange(slots, dtype=f32)[None, :, None]) & (
        mask_et[:, None, :] > 0.5
    )
    place_low = place.astype(bf16).reshape(experts * slots, rows)
    own_columns = lax.dynamic_slice_in_dim(cotangent, tp * quarter, quarter, axis=1)
    g_out = dot_plain(place_low, own_columns).astype(bf16).reshape(experts, slots, quarter)

    heads_out, lse, kv, notes, attn_part = kernel_call(
        "attn_forward",
        lambda *refs: attn_forward_kernel(heads, *refs),
        (idx, query, start, w_out, *along_y, *across),
        [SMEM] + [VMEM] * 11,
        (
            struct((rows, qw), bf16),
            struct((8, qw), f32),
            struct((all_tokens, 2 * HEAD_DIM), bf16),
            struct((ep_count * 16, 128), bf16),
            struct((rows, width), bf16),
        ),
        (VMEM,) * 5,
        flops=4 * 2048 * 128 * qw,
        moved=12 * MIB,
    )
    g_out, attn_part = lax.optimization_barrier((g_out, attn_part))
    g_mine = exchange_ep(g_out).reshape(-1, quarter)

    x1, h2_own = kernel_call(
        "mid_norm",
        mid_norm_kernel,
        (idx, own_tokens, ffn_row, attn_part, *tp_pieces(attn_part, tp)),
        [SMEM] + [VMEM] * 6,
        (struct((own, width), f32), struct((own, width), bf16)),
        (VMEM, VMEM),
        moved=2 * MIB,
    )

    h2 = kernel_call(
        "rows_all",
        assemble_kernel,
        (idx, h2_own, *tp_spread(h2_own)),
        [SMEM] + [VMEM] * 4,
        struct((rows, width), bf16),
        VMEM,
        moved=2 * MIB,
    )
    g_mine, h2 = lax.optimization_barrier((g_mine, h2))
    h2_all = lax.all_gather(h2, EP, axis=0, tiled=True)
    g_in, u = cotangent_rows(idx, tp_quarters(tp_neighbours(g_mine)), expert_down[0])
    chosen = jnp.sum(
        (notes.reshape(ep_count, 16, rows)[:, 1 : 1 + top].astype(f32) == ep.astype(f32)).astype(
            f32
        ),
        axis=1,
    )
    places = jnp.where(chosen > 0.5, dot_plain(chosen.astype(bf16), before.astype(bf16)), -1.0)

    logits_et = lax.dot_general(
        w_router, h2, (((0,), (1,)), ((), ())), preferred_element_type=f32
    )
    masked = jnp.where(mask_et > 0.5, logits_et, masked_score)
    expo = jnp.where(
        mask_et > 0.5, jnp.exp(masked - jnp.max(masked, axis=0, keepdims=True)), 0.0
    )
    gate_et = expo / jnp.sum(expo, axis=0, keepdims=True)
    placed_gate = jnp.where(place, gate_et[:, None, :], 0.0)
    combine = placed_gate.astype(bf16).reshape(experts * slots, rows)
    gate_slots = jnp.sum(placed_gate, axis=2)
    gate_slots = jnp.pad(gate_slots, ((0, 0), (0, 128 - slots)))
    gate_sent = jnp.broadcast_to(gate_slots[:, None, :], (experts, 8, 128))

    shared_act, d_shared_g, d_shared_u, shared_out, d_two_shared = shared_experts(
        h2, cotangent, shared_gate, shared_up, shared_down
    )
    shared_grads = weight_grads(
        "shared_grads", [(h2, [d_shared_g, d_shared_u]), (cotangent, [shared_act])]
    )
    w_both = jnp.concatenate([expert_gate[0], expert_up[0]], axis=1)

    w_turned = lax.dynamic_slice_in_dim(
        jnp.concatenate([w_both, w_both], axis=0), tp * quarter, width, axis=0
    )

    gate_in = exchange_ep(gate_sent)[:, 0, :slots].reshape(-1, 1)
    h2_all, places, u, gate_in, w_both, w_turned = lax.optimization_barrier(
        (h2_all, places, u, gate_in, w_both, w_turned)
    )
    h2_all, combine, shared_out, d_two_shared, shared_grads = lax.optimization_barrier(
        (h2_all, combine, shared_out, d_two_shared, shared_grads)
    )
    shared_sum = lax.psum_scatter(shared_grads, EP, scatter_dimension=0, tiled=True)
    h2_in, act, gated_act, d_both, rider, *d_pieces = expert_main(
        h2_all, places, u, gate_in, w_both, w_turned, quarter
    )
    ff = act.shape[1]
    d_parts = tp_sum_quarters(*d_pieces)
    one, two = [part.reshape(ep_count, slots, -1) for part in expert_out(act, expert_down[0])]
    one = exchange_ep(one)
    d_rows = quarter_sum(d_parts, rider)
    d_rows, one = lax.optimization_barrier((d_rows, one))
    d_back = exchange_ep(d_rows.reshape(ep_count, slots, quarter + RIDER))
    d_back = d_back.reshape(-1, quarter + RIDER)
    expert_down_grad = dot_first(gated_act, g_in)[None]
    expert_gate_grad = dot_first(h2_in, d_both[:, :ff])[None]
    expert_up_grad = dot_first(h2_in, d_both[:, ff:])[None]
    d_back, expert_down_grad, expert_gate_grad, expert_up_grad = lax.optimization_barrier(
        (d_back, expert_down_grad, expert_gate_grad, expert_up_grad)
    )

    d_two_part, d_logits_et = combine_call(
        idx, place_low, gate_et, d_back, d_two_shared, w_router.T
    )
    two, d_two_part = lax.optimization_barrier((two, d_two_part))
    two = exchange_ep(two)
    d_x1, d_attn_own, ffn_part = kernel_call(
        "mid_backward",
        mid_backward_kernel,
        (idx, d_two_part, *tp_pieces(d_two_part, tp), x1, ffn_row, own_cot),
        [SMEM] + [VMEM] * 7,
        (struct((own, width), f32), struct((own, width), bf16), struct((8, width), f32)),
        (VMEM,) * 3,
        moved=2 * MIB,
    )

    d_attn_far, two = lax.optimization_barrier((tp_spread(d_attn_own), two))
    d_attn, d_query_raw, d_kv = kernel_call(
        "attn_backward",
        lambda *refs: attn_backward_kernel(heads, *refs),
        (idx, query, heads_out, lse, kv, notes, start, turn, w_out)
        + (d_attn_own, *d_attn_far),
        [SMEM] + [VMEM] * 12,
        (
            struct((rows, width), bf16),
            struct((rows, qw), bf16),
            struct((all_tokens, 2 * HEAD_DIM), bf16),
        ),
        (VMEM,) * 3,
        flops=10 * 2048 * 128 * qw,
        moved=12 * MIB,
    )
    out_query_grads = weight_grads(
        "out_query_grads", [(d_attn, [heads_out]), (h1, [d_query_raw])]
    )
    out_query_grads, shared_sum = lax.optimization_barrier((out_query_grads, shared_sum))
    out_query_sum = lax.psum_scatter(out_query_grads, EP, scatter_dimension=0, tiled=True)
    d_kv = exchange_ep(d_kv.reshape(ep_count, rows, 2 * HEAD_DIM))
    d_one_query = dot_last(d_query_raw, w_query)
    d_kv, d_one_query = lax.optimization_barrier((d_kv, d_one_query))
    d_key_raw, d_value, d_one_part, attn_part_sum = kernel_call(
        "first_backward",
        first_backward_kernel,
        (d_kv, turn, key_weight, value_weight, d_one_query, tokens),
        [VMEM] * 6,
        (
            struct((rows, HEAD_DIM), bf16),
            struct((rows, HEAD_DIM), bf16),
            struct((rows, width), bf16),
            struct((8, width), f32),
        ),
        (VMEM,) * 4,
        flops=4 * rows * width * HEAD_DIM,
        moved=8 * MIB,
    )
    input_own = kernel_call(
        "input_rows",
        input_rows_kernel,
        (idx, d_one_part, *tp_pieces(d_one_part, tp), own_tokens, attn_row, d_x1),
        [SMEM] + [VMEM] * 7,
        struct((own, width), bf16),
        VMEM,
        moved=2 * MIB,
    )
    input_grad = kernel_call(
        "input_all",
        assemble_kernel,
        (idx, input_own, *tp_spread(input_own)),
        [SMEM] + [VMEM] * 4,
        struct((rows, width), f32),
        VMEM,
        moved=2 * MIB,
    )

    d_logits_all = tp_sum_small(d_logits_et).T.astype(bf16)
    d_logits_all = jnp.pad(d_logits_all, ((0, 0), (0, 128 - experts)))
    attn_total = tp_sum_small(attn_part_sum[0:1])
    ffn_total = tp_sum_small(ffn_part[0:1])
    attn_high, ffn_high = attn_total.astype(bf16), ffn_total.astype(bf16)
    gains = jnp.concatenate(
        [
            attn_high,
            ffn_high,
            (attn_total - attn_high.astype(f32)).astype(bf16),
            (ffn_total - ffn_high.astype(f32)).astype(bf16),
            jnp.zeros((12, width), bf16),
        ],
        axis=0,
    )
    pick = (
        jnp.arange(16, dtype=jnp.int32)[:, None] + experts
        == jnp.arange(128, dtype=jnp.int32)[None, :]
    ).astype(bf16)

    def strip(height):
        return pl.BlockSpec((height, GRAD_ROWS), lambda i: (0, i))

    small = kernel_call(
        "small_grads",
        small_grad_kernel,
        (h1, d_key_raw, d_value, h2, d_logits_all, gains, pick),
        [strip(rows), fixed((rows, 128)), fixed((rows, 128)), strip(rows), fixed((rows, 128))]
        + [strip(16), fixed((16, 128))],
        struct((width, 384), bf16),
        pl.BlockSpec((GRAD_ROWS, 384), lambda i: (i, 0)),
        flops=2 * rows * width * 384,
        moved=3 * MIB,
        grid=(width // GRAD_ROWS,),
    )
    small = exchange_ep(small.reshape(ep_count, width // ep_count, 384))
    small = jnp.sum(small.astype(f32), axis=0)
    gain_at = 2 * HEAD_DIM + experts

    one, two = [part.reshape(ep_count * slots, -1) for part in (one, two)]
    out_part = output_part(combine, one, two, shared_out)
    output_own = kernel_call(
        "output_rows",
        output_rows_kernel,
        (idx, out_part, *tp_pieces(out_part, tp), x1),
        [SMEM] + [VMEM] * 5,
        struct((own, width), bf16),
        VMEM,
        moved=2 * MIB,
    )
    output = kernel_call(
        "output_all",
        assemble_kernel,
        (idx, output_own, *tp_spread(output_own)),
        [SMEM] + [VMEM] * 4,
        struct((rows, width), bf16),
        VMEM,
        moved=2 * MIB,
    )

    sff = shared_act.shape[1]
    return (
        output,
        input_grad,
        small[:, gain_at] + small[:, gain_at + 2],
        out_query_sum[:, qw:].astype(f32),
        small[:, :HEAD_DIM],
        small[:, HEAD_DIM : 2 * HEAD_DIM],
        out_query_sum[:, :qw].astype(f32).T,
        small[:, gain_at + 1] + small[:, gain_at + 3],
        small[:, 2 * HEAD_DIM : gain_at],
        shared_sum[:, :sff].astype(f32),
        shared_sum[:, sff : 2 * sff].astype(f32),
        shared_sum[:, 2 * sff :].astype(f32).T,
        expert_gate_grad,
        expert_up_grad,
        expert_down_grad,
    )


def solution(mesh):
    ep_count, tp_count = mesh.shape["ep"], mesh.shape["tp"]
    side = math.isqrt(ep_count // 2)
    grid = Mesh(mesh.devices.reshape(side, side, 2, tp_count), EP + (TP,))
    return jax.shard_map(
        body,
        mesh=grid,
        in_specs=(
            P(EP, None),
            P(EP),
            P(EP, None),
            P(EP, None),
            P(),
            P(None, TP),
            P(None, TP),
            P(None, TP),
            P(TP, None),
            P(),
            P(),
            P(None, TP),
            P(None, TP),
            P(TP, None),
            P(EP, None, TP),
            P(EP, None, TP),
            P(EP, TP, None),
        ),
        out_specs=(
            P(EP, None),
            P(EP, None),
            P(EP),
            P(EP, TP),
            P(EP, TP),
            P(EP, TP),
            P(TP, EP),
            P(EP),
            P(EP, None),
            P(EP, TP),
            P(EP, TP),
            P(TP, EP),
            P(EP, None, TP),
            P(EP, None, TP),
            P(EP, TP, None),
        ),
        check_vma=False,
    )
```
